32 devices in a mesh: ccd: 4 (over y, core), tile: 8 (over z, x).
Axes of the slice: x: 2, y: 2, z: 4, core: 2. Of those that a mesh axis runs over, the one named last changes fastest.
Arguments:
- exposures: float32 [8, 2048, 4096], P('tile', 'ccd'), may hold values from -6 to 6
- interp: bfloat16 [8, 32, 256, 128], P('tile'), may hold values from -0.375 to 0.375
- col_offsets: int32 [8, 32], P('tile'), may hold values from 0 to 30
- template: float32 [2048, 4096], P('ccd', 'tile'), may hold values from -6 to 6
- coef_table: float32 [8, 4, 3, 3], replicated, may hold values from -3 to 3
- coef_index: int32 [8, 4, 8], replicated, may hold values from 0 to 3
- intersection: int32 [8, 4, 8], replicated, may hold values 0 or 1
Outputs:
- difference: float32 [8, 2048, 4096], P('tile', 'ccd')
The draws below stay inside these ranges and needn't reach their ends.
All inputs are finite; a program needn't handle non-finite values.
Results may differ from the reference program's by a relative error of at most 0.0029.
Values sent between devices are 32-bit elements; how exact they have to be, the bound alone decides.
A program may use at most 128 MiB of HBM per device.

```python
import jax
import jax.numpy as jnp
from jax import lax

COLS = 4096
ROWS_DEV = 512
BLOCK = 128
HALF = 10
KSETS = 4
EXPOSURES = 8
SKY_ROWS = 2048
PATCH_COLS = 512
BLOCKS = 32
PR_COUNT = 4
PC_COUNT = 8


def touch_ends(values, own_key, low, largest):
    longest = values.shape.index(max(values.shape))
    spots = []
    for shift in (0, 1):
        where = [jax.random.randint(jax.random.fold_in(own_key, axis), (), 0, length) for axis, length in enumerate(values.shape)]
        where[longest] = (where[longest] + shift) % values.shape[longest]
        spots.append(tuple(where))
    return values.at[spots[0]].set(low).at[spots[1]].set(largest)


def block_scale(rng, shape, cuts, least, high):
    gain = 1.0
    for position, parts in cuts:
        steps = jax.random.uniform(jax.random.fold_in(jax.random.fold_in(rng, 6), position), (parts,), jnp.float32, least / len(cuts), high / len(cuts))
        gain = gain * jnp.repeat(jnp.exp(steps), shape[position] // parts).reshape((-1,) + (1,) * (len(shape) - 1 - position))
    return gain


def scatter_about(key, extent, spread, most, shards=(), kind=jnp.bfloat16):
    values = spread * jax.random.normal(key, extent, jnp.float32)
    if shards:
        values = values * block_scale(key, extent, shards, -0.22, 0.18)
    return jnp.clip(values, -most, most).astype(kind)


def setup_inputs(seed: int = 0) -> dict:
    keys = jax.random.split(jax.random.key(seed), 8)
    return {
        "exposures": scatter_about(keys[0], (EXPOSURES, SKY_ROWS, COLS), 1.0, 6.0, ((0, 8), (1, 4)), jnp.float32),
        "interp": scatter_about(keys[1], (EXPOSURES, BLOCKS, 2 * BLOCK, BLOCK), (2 * BLOCK) ** -0.5, 0.375, ((0, 8),)),
        "col_offsets": touch_ends(jax.random.randint(keys[2], (EXPOSURES, BLOCKS), 0, BLOCKS - 1), jax.random.fold_in(keys[2], 1), 0, (BLOCKS - 1) - 1).astype(jnp.int32),
        "template": scatter_about(keys[3], (SKY_ROWS, COLS), 1.0, 6.0, ((0, 4), (1, 8)), jnp.float32),
        "coef_table": scatter_about(keys[4], (EXPOSURES, KSETS, 3, 3), 0.5, 3.0, (), jnp.float32),
        "coef_index": touch_ends(jax.random.randint(keys[5], (EXPOSURES, PR_COUNT, PC_COUNT), 0, KSETS), jax.random.fold_in(keys[5], 1), 0, KSETS - 1).astype(jnp.int32),
        "intersection": touch_ends((jax.random.randint(keys[6], (EXPOSURES, PR_COUNT, PC_COUNT), 0, 4) < 3).astype(jnp.int32), jax.random.fold_in(keys[6], 1), 0, 1),
    }


SIGMAS = (1.5, 3.0, 5.0)


def basis_taps(half_width):
    positions = jnp.arange(-half_width, half_width + 1).astype(jnp.float32)
    kernels = []
    for sigma_value in SIGMAS:
        gauss = jnp.exp(-0.5 * (positions / sigma_value) ** 2)
        kernels.append(gauss / jnp.sum(gauss))
    return kernels


def smooth(padded, gauss, out_rows, out_cols):
    tap_count = gauss.shape[0]
    across = gauss[0] * padded[0:out_rows, :]
    for offset in range(1, tap_count):
        across = across + gauss[offset] * padded[offset:offset + out_rows, :]
    result = gauss[0] * across[:, 0:out_cols]
    for offset in range(1, tap_count):
        result = result + gauss[offset] * across[:, offset:offset + out_cols]
    return result


def resample(exposure_img, weights, offsets):
    row_count = exposure_img.shape[0]
    tiles = exposure_img.astype(jnp.bfloat16).reshape(row_count, BLOCKS, BLOCK)
    first_part = jnp.take(tiles, offsets, axis=1)
    second_part = jnp.take(tiles, offsets + 1, axis=1)
    window = jnp.concatenate([first_part, second_part], axis=2)
    output = jnp.einsum("rjk,jkn->rjn", window.astype(jnp.float32), weights.astype(jnp.float32))
    return output.reshape(row_count, BLOCKS * BLOCK)


def expand(grid):
    return jnp.repeat(jnp.repeat(grid, ROWS_DEV, axis=0), PATCH_COLS, axis=1)


def reference(exposures, interp, col_offsets, template, coef_table, coef_index, intersection):
    kernels = basis_taps(HALF)
    padded = jnp.pad(template, HALF)
    smoothed = [smooth(padded, gauss, SKY_ROWS, COLS) for gauss in kernels]
    row_coord = ((jnp.arange(SKY_ROWS) % ROWS_DEV).astype(jnp.float32) - (ROWS_DEV - 1) / 2.0) / (ROWS_DEV / 2.0)
    col_coord = ((jnp.arange(COLS) % PATCH_COLS).astype(jnp.float32) - (PATCH_COLS - 1) / 2.0) / (PATCH_COLS / 2.0)

    def visit(operands):
        exposure_img, weights, offsets, table, indices, covered = operands
        warped = resample(exposure_img, weights, offsets)
        set_pick = (indices[:, :, None] == jnp.arange(KSETS)[None, None, :]).astype(jnp.float32)
        kernel_coef = jnp.sum(set_pick[:, :, :, None, None] * table[None, None], axis=2)
        template_model = None
        for kernel_index in range(3):
            pieces = [expand(kernel_coef[:, :, kernel_index, component]) for component in range(3)]
            weight_map = (pieces[0] + pieces[1] * col_coord[None, :]) + pieces[2] * row_coord[:, None]
            contrib = weight_map * smoothed[kernel_index]
            template_model = contrib if template_model is None else template_model + contrib
        coverage = expand(covered.astype(jnp.float32))
        return (warped - template_model) * coverage

    return lax.map(visit, (exposures, interp, col_offsets, coef_table, coef_index, intersection))
```

```python
import functools
import heapq

import jax
import jax.numpy as jnp
import ml_dtypes
import numpy as np
from jax import lax
from jax.experimental import pallas as pl
from jax.experimental.pallas import tpu as pltpu
from jax.sharding import PartitionSpec as P

HALF = 10
KSETS = 4
SIGMAS = (1.5, 3.0, 5.0)
HALO = 16
EDGE = 128
BAND = 128
CHUNKS = 2
LINES = 128
STORES = 8


def basis_taps():
    positions = np.arange(-HALF, HALF + 1).astype(np.float64)
    kernels = []
    for sigma_value in SIGMAS:
        gauss = np.exp(-0.5 * (positions / sigma_value) ** 2)
        kernels.append(gauss / np.sum(gauss))
    return kernels


def smoothing_gains():
    near = [taps.astype(ml_dtypes.bfloat16).astype(np.float64) for taps in basis_taps()]
    return [1.0 / np.sum(taps) ** 2 for taps in near]


def banded(b, rows, cols, shift, first=0):
    shape = (rows, cols)
    distance = (
        lax.broadcasted_iota(jnp.int32, shape, 1)
        - lax.broadcasted_iota(jnp.int32, shape, 0)
        - (shift + first)
    )
    away = distance.astype(jnp.float32)
    taps = jnp.exp(away * away * (-0.5 / SIGMAS[b] ** 2)) * basis_taps()[b][HALF]
    return jnp.where(jnp.abs(away) <= HALF, taps, 0.0).astype(jnp.bfloat16)


def inner_size(count):
    best = 1
    for size in range(1, count + 1):
        if count % size == 0 and size * size <= count:
            best = size
    return best


def turns(d, qz, c, outer):
    late = c >= CHUNKS // 2
    ends = ((d == 0) & (qz == outer - 1)) | ((d == outer - 1) & (qz == 0))
    inside = (d > 0) & (d < outer - 1) & ((qz == d - 1) | (qz == d + 1))
    return (ends & late) | (inside & (late | (qz == 0) | (qz == outer - 1)))


def paths(me, q, c, count):
    inner = inner_size(count)
    outer = count // inner
    z, x = me // inner, me % inner
    qz, qx = q // inner, q % inner
    own = qx == x
    across = (qz == z) | (turns(z, qz, c, outer) ^ True)
    return (
        (z > 0) & (qz >= z) & (own | turns(z - 1, qz, c, outer)),
        (z < outer - 1) & (qz <= z) & (own | turns(z + 1, qz, c, outer)),
        across & (qx >= x) & (x > 0),
        across & (qx <= x) & (x < inner - 1),
    )


def arrival_events(count):
    inner = inner_size(count)
    steps = (-inner, inner, -1, 1)
    free, order = {}, 0
    queue = [(0, False, me, me, c, me * CHUNKS + c) for me in range(count) for c in range(CHUNKS)]
    order = len(queue)
    heapq.heapify(queue)
    events = [[] for _ in range(count)]
    while queue:
        time, _, me, q, c, _ = heapq.heappop(queue)
        if q != me:
            events[me].append(q * CHUNKS + c)
        for d, go in enumerate(paths(me, q, c, count)):
            if go:
                done = max(free.get((me, d), 0), time) + 1
                free[me, d] = done
                to = me + steps[d]
                heapq.heappush(queue, (done, (q - to) % inner != 0, to, q, c, order))
                order += 1
    return events


DIGIT = 256
PER_WORD = 3


def arrival_codes(count):
    codes = []
    for events in arrival_events(count):
        assert len(events) == (count - 1) * CHUNKS
        left = {q: CHUNKS for q in range(count)}
        digits = []
        for event in events:
            left[event // CHUNKS] -= 1
            digits.append(event * 2 + (left[event // CHUNKS] == 0))
        codes.append([
            sum(int(v) * DIGIT**i for i, v in enumerate(digits[first : first + PER_WORD]))
            for first in range(0, len(digits), PER_WORD)
        ])
    return codes


def strip_kernel(
    count, ccd_count, template, exposure, interp, offset_in, coef_in, index_in, cover_in, out,
    strip, down, across, weights, lines, pixels, mats, offsets, coef, index, cover,
    load_sem, line_sem, small_sem, send_sem, recv_sem, hsend_sem, hrecv_sem,
):
    me = lax.axis_index("tile")
    row = lax.axis_index("ccd")
    inner = inner_size(count)
    outer = count // inner
    z, x = me // inner, me % inner
    rows, patch_cols = template.shape
    cols = out.shape[1]
    part = rows // CHUNKS

    targets = (me - inner, me + inner, me - 1, me + 1)
    there = (z > 0, z < outer - 1, x > 0, x < inner - 1)
    halo_there = (row > 0, row < ccd_count - 1)

    barrier = pltpu.get_barrier_semaphore()
    total = jnp.int32(0)
    for target, exists in zip(targets, there):
        @pl.when(exists)
        def _():
            pl.semaphore_signal(barrier, inc=1, device_id=(row, target))
        total = total + exists.astype(jnp.int32)
    for step, exists in zip((-1, 1), halo_there):
        @pl.when(exists)
        def _():
            pl.semaphore_signal(barrier, inc=1, device_id=(row + step, me))
        total = total + exists.astype(jnp.int32)

    load = pltpu.make_async_copy(template, strip.at[me, pl.ds(HALO, rows)], load_sem)
    load.start()
    small = [
        pltpu.make_async_copy(source, target, small_sem.at[i])
        for i, (source, target) in enumerate(
            [(offset_in, offsets), (coef_in, coef), (index_in, index), (cover_in, cover), (interp, mats)]
        )
    ]
    for copy in small:
        copy.start()

    def line_copy(i, slot):
        return pltpu.make_async_copy(
            exposure.at[pl.ds(pl.multiple_of(i * LINES, LINES), LINES)], lines.at[slot], line_sem.at[slot]
        )

    line_copy(0, 0).start()
    pl.semaphore_wait(barrier, total)

    def send(q, c, d, own):
        piece = pl.ds(pl.multiple_of(HALO + c * part, HALO), part)
        return pltpu.make_async_remote_copy(
            src_ref=template.at[pl.ds(c * part, part)] if own else strip.at[q, piece],
            dst_ref=strip.at[q, piece],
            send_sem=send_sem.at[d, q, c],
            recv_sem=recv_sem.at[q, c],
            device_id=(row, targets[d]),
        )

    def halo(q, d):
        source = pl.ds(HALO, HALO) if d == 0 else pl.ds(rows, HALO)
        target = pl.ds(HALO + rows, HALO) if d == 0 else pl.ds(0, HALO)
        return pltpu.make_async_remote_copy(
            src_ref=strip.at[q, source],
            dst_ref=strip.at[q, target],
            send_sem=hsend_sem.at[d, q],
            recv_sem=hrecv_sem.at[d, q],
            device_id=(row + (-1 if d == 0 else 1), me),
        )

    for c in range(CHUNKS):
        for d in range(4):
            @pl.when(there[d])
            def _():
                send(me, c, d, True).start()
    load.wait()
    for d in range(2):
        @pl.when(halo_there[d])
        def _():
            halo(me, d).start()

    @pl.when(row == 0)
    def _():
        for q in range(count):
            strip[q, 0:HALO, :] = jnp.zeros((HALO, patch_cols), jnp.float32)

    @pl.when(row == ccd_count - 1)
    def _():
        for q in range(count):
            strip[q, rows + HALO : rows + 2 * HALO, :] = jnp.zeros((HALO, patch_cols), jnp.float32)

    for copy in small:
        copy.wait()

    blocks, depth, block = mats.shape

    def warp(i, carry):
        slot = i % 2
        line_copy(i, slot).wait()

        @pl.when(i + 1 < rows // LINES)
        def _():
            line_copy(i + 1, 1 - slot).start()

        for j in range(blocks):
            pixels[j] = lines[slot, :, j * block : (j + 1) * block].astype(jnp.bfloat16)
        here = pl.ds(pl.multiple_of(i * LINES, LINES), LINES)
        for j in range(blocks):
            start = offsets[j]
            window = [pixels[start + k] for k in range(depth // block)]
            value = jnp.dot(
                jnp.concatenate(window, axis=1), mats[j], preferred_element_type=jnp.float32
            )
            covered = cover[me * (ccd_count * count) + row * count + j * block // patch_cols]
            out[here, j * block : (j + 1) * block] = value * covered.astype(jnp.float32)
        return carry

    lax.fori_loop(0, rows // LINES, warp, 0)

    gains = smoothing_gains()
    u = (
        lax.broadcasted_iota(jnp.int32, (1, patch_cols), 1).astype(jnp.float32) * (2.0 / patch_cols)
        - (patch_cols - 1) / patch_cols
    )
    weights[...] = jnp.zeros(weights.shape, jnp.float32)
    for q in range(count):
        spot = me * (ccd_count * count) + row * count + q
        chosen = index[spot]
        covered = cover[spot].astype(jnp.float32)
        here = slice(EDGE + q * patch_cols, EDGE + (q + 1) * patch_cols)
        for b in range(3):
            terms = []
            for k in range(3):
                sets = [coef[me * (KSETS * 9) + i * 9 + b * 3 + k] for i in range(KSETS)]
                term = sets[0]
                for i in range(1, KSETS):
                    term = jnp.where(chosen == i, sets[i], term)
                terms.append(term * covered * float(gains[b]))
            const, slope, lift = terms
            weights[b : b + 1, here] = const + slope * u
            weights[3 + b : 4 + b, here] = jnp.full((1, patch_cols), lift, jnp.float32)

    def add_model(q):
        first = pl.multiple_of(q * patch_cols, EDGE)
        wide = patch_cols + 2 * EDGE
        left = pl.multiple_of(jnp.maximum(first - EDGE, 0), EDGE)
        right = pl.multiple_of(jnp.minimum(first + patch_cols, cols - EDGE), EDGE)

        def band(r, carry):
            at = pl.multiple_of(r * BAND, BAND)
            here = pl.ds(at, BAND)
            pixel = strip[q, pl.ds(at, BAND + 2 * HALO), :].astype(jnp.bfloat16)
            tall = jnp.dot(down[...], pixel, preferred_element_type=jnp.float32)
            tall = tall.astype(jnp.bfloat16)
            v = (
                lax.broadcasted_iota(jnp.int32, (BAND, wide), 0) + r * BAND
            ).astype(jnp.float32) * (2.0 / rows) - (rows - 1) / rows
            model = None
            for b in range(3):
                flat = jnp.dot(
                    tall[b * BAND : (b + 1) * BAND], across[b], preferred_element_type=jnp.float32
                )
                const = weights[b : b + 1, pl.ds(first, wide)]
                slope = weights[3 + b : 4 + b, pl.ds(first, wide)]
                term = (const + slope * v) * flat
                model = term if model is None else model + term
            out[here, pl.ds(first, patch_cols)] -= model[:, EDGE : EDGE + patch_cols]
            out[here, pl.ds(left, EDGE)] -= model[:, :EDGE]
            out[here, pl.ds(right, EDGE)] -= model[:, EDGE + patch_cols :]
            return carry

        lax.fori_loop(0, rows // BAND, band, 0)

    def halos_in(q):
        for d in range(2):
            @pl.when(halo_there[1 - d])
            def _():
                halo(q, d).wait_recv()

    for b in range(3):
        down[b * BAND : (b + 1) * BAND, :] = banded(b, BAND, BAND + 2 * HALO, HALO)

        def fill(i, carry):
            first = pl.multiple_of(i * HALO, HALO)
            across[b, pl.ds(first, HALO), :] = banded(
                b, HALO, patch_cols + 2 * EDGE, EDGE, i * HALO
            )
            return carry

        lax.fori_loop(0, patch_cols // HALO, fill, 0)

    halos_in(me)
    add_model(me)

    table = arrival_codes(count)
    words = []
    for w in range(len(table[0])):
        word = jnp.int32(0)
        for i in range(count):
            word = jnp.where(me == i, jnp.int32(table[i][w]), word)
        words.append(word)

    def arrive(_, words):
        words = list(words)
        digit = words[0] % DIGIT
        for w in range(len(words)):
            words[w] = words[w] // DIGIT
            if w + 1 < len(words):
                words[w] = words[w] + (words[w + 1] % DIGIT) * DIGIT ** (PER_WORD - 1)
        done, event = digit % 2, digit // 2
        q, c = event // CHUNKS, event % CHUNKS
        send(q, c, 0, False).wait_recv()
        onward = paths(me, q, c, count)
        for d in range(4):
            @pl.when(onward[d])
            def _():
                send(q, c, d, False).start()
        for d in range(2):
            @pl.when((c == (0 if d == 0 else CHUNKS - 1)) & halo_there[d])
            def _():
                halo(q, d).start()

        @pl.when(done == 1)
        def _():
            halos_in(q)
            add_model(q)

        return tuple(words)

    lax.fori_loop(0, (count - 1) * CHUNKS, arrive, tuple(words))

    def drain(event, carry):
        q, c = event // CHUNKS, event % CHUNKS
        onward = paths(me, q, c, count)
        for d in range(4):
            @pl.when(onward[d])
            def _():
                send(q, c, d, False).wait_send()
        for d in range(2):
            @pl.when((c == 0) & halo_there[d])
            def _():
                halo(q, d).wait_send()
        return carry

    lax.fori_loop(0, count * CHUNKS, drain, 0)


def store_kernel(value, out, sem):
    rows = value.shape[0] // STORES
    copies = [
        pltpu.make_async_copy(value.at[pl.ds(i * rows, rows)], out.at[pl.ds(i * rows, rows)], sem.at[i])
        for i in range(STORES)
    ]
    for copy in copies:
        copy.start()
    for copy in copies:
        copy.wait()


def on_device(exposures, interp, col_offsets, template, coef_table, coef_index, intersection):
    rows, cols = exposures.shape[1:]
    patch_cols = template.shape[1]
    count, ccd_count = lax.axis_size("tile"), lax.axis_size("ccd")
    blocks, depth, block = interp.shape[1:]
    small = [coef_table.reshape(-1), coef_index.reshape(-1), intersection.reshape(-1)]

    in_hbm = pl.BlockSpec(memory_space=pltpu.HBM)
    vmem = pl.BlockSpec(memory_space=pltpu.VMEM)
    value = pl.pallas_call(
        functools.partial(strip_kernel, count, ccd_count),
        out_shape=jax.ShapeDtypeStruct((rows, cols), jnp.float32),
        in_specs=[in_hbm] * 7,
        out_specs=vmem,
        scratch_shapes=[
            pltpu.VMEM((count, rows + 2 * HALO, patch_cols), jnp.float32),
            pltpu.VMEM((3 * BAND, BAND + 2 * HALO), jnp.bfloat16),
            pltpu.VMEM((3, patch_cols, patch_cols + 2 * EDGE), jnp.bfloat16),
            pltpu.VMEM((8, cols + 2 * EDGE), jnp.float32),
            pltpu.VMEM((2, LINES, cols), jnp.float32),
            pltpu.VMEM((blocks, LINES, block), jnp.bfloat16),
            pltpu.VMEM((blocks, depth, block), jnp.bfloat16),
            pltpu.SMEM((blocks,), jnp.int32),
            *[pltpu.SMEM(array.shape, array.dtype) for array in small],
            pltpu.SemaphoreType.DMA,
            pltpu.SemaphoreType.DMA((2,)),
            pltpu.SemaphoreType.DMA((5,)),
            pltpu.SemaphoreType.DMA((4, count, CHUNKS)),
            pltpu.SemaphoreType.DMA((count, CHUNKS)),
            pltpu.SemaphoreType.DMA((2, count)),
            pltpu.SemaphoreType.DMA((2, count)),
        ],
        compiler_params=pltpu.CompilerParams(
            collective_id=0, has_side_effects=True, vmem_limit_bytes=40 * 2**20
        ),
    )(template, exposures[0], interp[0], col_offsets[0], *small)
    result = pl.pallas_call(
        store_kernel,
        out_shape=jax.ShapeDtypeStruct((rows, cols), jnp.float32),
        in_specs=[vmem],
        out_specs=in_hbm,
        scratch_shapes=[pltpu.SemaphoreType.DMA((STORES,))],
        compiler_params=pltpu.CompilerParams(vmem_limit_bytes=2**20),
    )(value)
    return result[None]


def solution(mesh):
    placed = (
        P("tile", "ccd", None),
        P("tile", None, None, None),
        P("tile", None),
        P("ccd", "tile"),
        P(),
        P(),
        P(),
    )
    return jax.shard_map(
        on_device, mesh=mesh, in_specs=placed, out_specs=P("tile", "ccd", None), check_vma=False
    )
```

```python
import functools
import heapq

import jax
import jax.numpy as jnp
import ml_dtypes
import numpy as np
from jax import lax
from jax.experimental import pallas as pl
from jax.experimental.pallas import tpu as pltpu
from jax.sharding import PartitionSpec as P

HALF = 10
KSETS = 4
SIGMAS = (1.5, 3.0, 5.0)
HALO = 16
EDGE = 128
BAND = 128
CHUNKS = 2
LINES = 128
STORES = 8


def basis_taps():
    positions = np.arange(-HALF, HALF + 1).astype(np.float64)
    kernels = []
    for sigma_value in SIGMAS:
        gauss = np.exp(-0.5 * (positions / sigma_value) ** 2)
        kernels.append(gauss / np.sum(gauss))
    return kernels


def smoothing_gains():
    near = [taps.astype(ml_dtypes.bfloat16).astype(np.float64) for taps in basis_taps()]
    return [1.0 / np.sum(taps) ** 2 for taps in near]


def banded(b, rows, cols, shift, first=0):
    shape = (rows, cols)
    distance = (
        lax.broadcasted_iota(jnp.int32, shape, 1)
        - lax.broadcasted_iota(jnp.int32, shape, 0)
        - (shift + first)
    )
    away = distance.astype(jnp.float32)
    taps = jnp.exp(away * away * (-0.5 / SIGMAS[b] ** 2)) * basis_taps()[b][HALF]
    return jnp.where(jnp.abs(away) <= HALF, taps, 0.0).astype(jnp.bfloat16)


def inner_size(count):
    best = 1
    for size in range(1, count + 1):
        if count % size == 0 and size * size <= count:
            best = size
    return best


def turns(d, qz, c, outer):
    late = c >= CHUNKS // 2
    ends = ((d == 0) & (qz == outer - 1)) | ((d == outer - 1) & (qz == 0))
    inside = (d > 0) & (d < outer - 1) & ((qz == d - 1) | (qz == d + 1))
    return (ends & late) | (inside & (late | (qz == 0) | (qz == outer - 1)))


def paths(me, q, c, count):
    inner = inner_size(count)
    outer = count // inner
    z, x = me // inner, me % inner
    qz, qx = q // inner, q % inner
    own = qx == x
    across = (qz == z) | (turns(z, qz, c, outer) ^ True)
    return (
        (z > 0) & (qz >= z) & (own | turns(z - 1, qz, c, outer)),
        (z < outer - 1) & (qz <= z) & (own | turns(z + 1, qz, c, outer)),
        across & (qx >= x) & (x > 0),
        across & (qx <= x) & (x < inner - 1),
    )


def arrival_events(count):
    inner = inner_size(count)
    steps = (-inner, inner, -1, 1)
    free, order = {}, 0
    queue = [(0, False, me, me, c, me * CHUNKS + c) for me in range(count) for c in range(CHUNKS)]
    order = len(queue)
    heapq.heapify(queue)
    events = [[] for _ in range(count)]
    while queue:
        time, _, me, q, c, _ = heapq.heappop(queue)
        if q != me:
            events[me].append(q * CHUNKS + c)
        for d, go in enumerate(paths(me, q, c, count)):
            if go:
                done = max(free.get((me, d), 0), time) + 1
                free[me, d] = done
                to = me + steps[d]
                heapq.heappush(queue, (done, (q - to) % inner != 0, to, q, c, order))
                order += 1
    return events


DIGIT = 256
PER_WORD = 3


def arrival_codes(count):
    codes = []
    for events in arrival_events(count):
        assert len(events) == (count - 1) * CHUNKS
        left = {q: CHUNKS for q in range(count)}
        digits = []
        for event in events:
            left[event // CHUNKS] -= 1
            digits.append(event * 2 + (left[event // CHUNKS] == 0))
        codes.append([
            sum(int(v) * DIGIT**i for i, v in enumerate(digits[first : first + PER_WORD]))
            for first in range(0, len(digits), PER_WORD)
        ])
    return codes


def strip_kernel(
    count, ccd_count, template, exposure, interp, offset_in, coef_in, index_in, cover_in, out,
    strip, down, across, weights, lines, pixels, mats, offsets, coef, index, cover,
    load_sem, line_sem, small_sem, send_sem, recv_sem, hsend_sem, hrecv_sem,
):
    me = lax.axis_index("tile")
    row = lax.axis_index("ccd")
    inner = inner_size(count)
    outer = count // inner
    z, x = me // inner, me % inner
    rows, patch_cols = template.shape
    cols = out.shape[1]
    part = rows // CHUNKS

    targets = (me - inner, me + inner, me - 1, me + 1)
    there = (z > 0, z < outer - 1, x > 0, x < inner - 1)
    halo_there = (row > 0, row < ccd_count - 1)

    barrier = pltpu.get_barrier_semaphore()
    total = jnp.int32(0)
    for target, exists in zip(targets, there):
        @pl.when(exists)
        def _():
            pl.semaphore_signal(barrier, inc=1, device_id=(row, target))
        total = total + exists.astype(jnp.int32)
    for step, exists in zip((-1, 1), halo_there):
        @pl.when(exists)
        def _():
            pl.semaphore_signal(barrier, inc=1, device_id=(row + step, me))
        total = total + exists.astype(jnp.int32)

    load = pltpu.make_async_copy(template, strip.at[me, pl.ds(HALO, rows)], load_sem)
    load.start()
    small = [
        pltpu.make_async_copy(source, target, small_sem.at[i])
        for i, (source, target) in enumerate(
            [(offset_in, offsets), (coef_in, coef), (index_in, index), (cover_in, cover), (interp, mats)]
        )
    ]
    for copy in small:
        copy.start()

    def line_copy(i, slot):
        return pltpu.make_async_copy(
            exposure.at[pl.ds(pl.multiple_of(i * LINES, LINES), LINES)], lines.at[slot], line_sem.at[slot]
        )

    line_copy(0, 0).start()
    pl.semaphore_wait(barrier, total)

    def send(q, c, d, own):
        piece = pl.ds(pl.multiple_of(HALO + c * part, HALO), part)
        return pltpu.make_async_remote_copy(
            src_ref=template.at[pl.ds(c * part, part)] if own else strip.at[q, piece],
            dst_ref=strip.at[q, piece],
            send_sem=send_sem.at[d, q, c],
            recv_sem=recv_sem.at[q, c],
            device_id=(row, targets[d]),
        )

    def halo(q, d):
        source = pl.ds(HALO, HALO) if d == 0 else pl.ds(rows, HALO)
        target = pl.ds(HALO + rows, HALO) if d == 0 else pl.ds(0, HALO)
        return pltpu.make_async_remote_copy(
            src_ref=strip.at[q, source],
            dst_ref=strip.at[q, target],
            send_sem=hsend_sem.at[d, q],
            recv_sem=hrecv_sem.at[d, q],
            device_id=(row + (-1 if d == 0 else 1), me),
        )

    for c in range(CHUNKS):
        for d in range(4):
            @pl.when(there[d])
            def _():
                send(me, c, d, True).start()
    load.wait()
    for d in range(2):
        @pl.when(halo_there[d])
        def _():
            halo(me, d).start()

    @pl.when(row == 0)
    def _():
        for q in range(count):
            strip[q, 0:HALO, :] = jnp.zeros((HALO, patch_cols), jnp.float32)

    @pl.when(row == ccd_count - 1)
    def _():
        for q in range(count):
            strip[q, rows + HALO : rows + 2 * HALO, :] = jnp.zeros((HALO, patch_cols), jnp.float32)

    for copy in small:
        copy.wait()

    blocks, depth, block = mats.shape

    def warp(i, carry):
        slot = i % 2
        line_copy(i, slot).wait()

        @pl.when(i + 1 < rows // LINES)
        def _():
            line_copy(i + 1, 1 - slot).start()

        for j in range(blocks):
            pixels[j] = lines[slot, :, j * block : (j + 1) * block].astype(jnp.bfloat16)
        here = pl.ds(pl.multiple_of(i * LINES, LINES), LINES)
        for j in range(blocks):
            start = offsets[0, j]
            window = [pixels[start + k] for k in range(depth // block)]
            value = jnp.dot(
                jnp.concatenate(window, axis=1), mats[j], preferred_element_type=jnp.float32
            )
            covered = cover[me, row, j * block // patch_cols]
            out[here, j * block : (j + 1) * block] = value * covered.astype(jnp.float32)
        return carry

    lax.fori_loop(0, rows // LINES, warp, 0)

    gains = smoothing_gains()
    u = (
        lax.broadcasted_iota(jnp.int32, (1, patch_cols), 1).astype(jnp.float32) * (2.0 / patch_cols)
        - (patch_cols - 1) / patch_cols
    )
    weights[...] = jnp.zeros(weights.shape, jnp.float32)
    for q in range(count):
        chosen = index[me, row, q]
        covered = cover[me, row, q].astype(jnp.float32)
        here = slice(EDGE + q * patch_cols, EDGE + (q + 1) * patch_cols)
        for b in range(3):
            terms = []
            for k in range(3):
                sets = [coef[b, k, i, me] for i in range(KSETS)]
                term = sets[0]
                for i in range(1, KSETS):
                    term = jnp.where(chosen == i, sets[i], term)
                terms.append(term * covered * float(gains[b]))
            const, slope, lift = terms
            weights[b : b + 1, here] = const + slope * u
            weights[3 + b : 4 + b, here] = jnp.full((1, patch_cols), lift, jnp.float32)

    def add_model(q):
        first = pl.multiple_of(q * patch_cols, EDGE)
        wide = patch_cols + 2 * EDGE
        left = pl.multiple_of(jnp.maximum(first - EDGE, 0), EDGE)
        right = pl.multiple_of(jnp.minimum(first + patch_cols, cols - EDGE), EDGE)

        def band(r, carry):
            at = pl.multiple_of(r * BAND, BAND)
            here = pl.ds(at, BAND)
            pixel = strip[q, pl.ds(at, BAND + 2 * HALO), :].astype(jnp.bfloat16)
            tall = jnp.dot(down[...], pixel, preferred_element_type=jnp.float32)
            tall = tall.astype(jnp.bfloat16)
            v = (
                lax.broadcasted_iota(jnp.int32, (BAND, wide), 0) + r * BAND
            ).astype(jnp.float32) * (2.0 / rows) - (rows - 1) / rows
            model = None
            for b in range(3):
                flat = jnp.dot(
                    tall[b * BAND : (b + 1) * BAND], across[b], preferred_element_type=jnp.float32
                )
                const = weights[b : b + 1, pl.ds(first, wide)]
                slope = weights[3 + b : 4 + b, pl.ds(first, wide)]
                term = (const + slope * v) * flat
                model = term if model is None else model + term
            out[here, pl.ds(first, patch_cols)] -= model[:, EDGE : EDGE + patch_cols]
            out[here, pl.ds(left, EDGE)] -= model[:, :EDGE]
            out[here, pl.ds(right, EDGE)] -= model[:, EDGE + patch_cols :]
            return carry

        lax.fori_loop(0, rows // BAND, band, 0)

    def halos_in(q):
        for d in range(2):
            @pl.when(halo_there[1 - d])
            def _():
                halo(q, d).wait_recv()

    for b in range(3):
        down[b * BAND : (b + 1) * BAND, :] = banded(b, BAND, BAND + 2 * HALO, HALO)

        def fill(i, carry):
            first = pl.multiple_of(i * HALO, HALO)
            across[b, pl.ds(first, HALO), :] = banded(
                b, HALO, patch_cols + 2 * EDGE, EDGE, i * HALO
            )
            return carry

        lax.fori_loop(0, patch_cols // HALO, fill, 0)

    halos_in(me)
    add_model(me)

    table = arrival_codes(count)
    words = []
    for w in range(len(table[0])):
        word = jnp.int32(0)
        for i in range(count):
            word = jnp.where(me == i, jnp.int32(table[i][w]), word)
        words.append(word)

    def arrive(_, words):
        words = list(words)
        digit = words[0] % DIGIT
        for w in range(len(words)):
            words[w] = words[w] // DIGIT
            if w + 1 < len(words):
                words[w] = words[w] + (words[w + 1] % DIGIT) * DIGIT ** (PER_WORD - 1)
        done, event = digit % 2, digit // 2
        q, c = event // CHUNKS, event % CHUNKS
        send(q, c, 0, False).wait_recv()
        onward = paths(me, q, c, count)
        for d in range(4):
            @pl.when(onward[d])
            def _():
                send(q, c, d, False).start()
        for d in range(2):
            @pl.when((c == (0 if d == 0 else CHUNKS - 1)) & halo_there[d])
            def _():
                halo(q, d).start()

        @pl.when(done == 1)
        def _():
            halos_in(q)
            add_model(q)

        return tuple(words)

    lax.fori_loop(0, (count - 1) * CHUNKS, arrive, tuple(words))

    def drain(event, carry):
        q, c = event // CHUNKS, event % CHUNKS
        onward = paths(me, q, c, count)
        for d in range(4):
            @pl.when(onward[d])
            def _():
                send(q, c, d, False).wait_send()
        for d in range(2):
            @pl.when((c == 0) & halo_there[d])
            def _():
                halo(q, d).wait_send()
        return carry

    lax.fori_loop(0, count * CHUNKS, drain, 0)


def store_kernel(value, out, sem):
    rows = value.shape[0] // STORES
    copies = [
        pltpu.make_async_copy(value.at[pl.ds(i * rows, rows)], out.at[pl.ds(i * rows, rows)], sem.at[i])
        for i in range(STORES)
    ]
    for copy in copies:
        copy.start()
    for copy in copies:
        copy.wait()


def on_device(exposures, interp, col_offsets, template, coef_table, coef_index, intersection):
    rows, cols = exposures.shape[1:]
    patch_cols = template.shape[1]
    count, ccd_count = lax.axis_size("tile"), lax.axis_size("ccd")
    blocks, depth, block = interp.shape[1:]
    small = [col_offsets, coef_table.transpose(2, 3, 1, 0), coef_index, intersection]

    sources = [
        pltpu.with_memory_space_constraint(array, pltpu.HBM)
        for array in (template, exposures[0], interp[0], *small)
    ]
    in_hbm = pl.BlockSpec(memory_space=pltpu.HBM)
    vmem = pl.BlockSpec(memory_space=pltpu.VMEM)
    value = pl.pallas_call(
        functools.partial(strip_kernel, count, ccd_count),
        out_shape=jax.ShapeDtypeStruct((rows, cols), jnp.float32),
        in_specs=[in_hbm] * 7,
        out_specs=vmem,
        scratch_shapes=[
            pltpu.VMEM((count, rows + 2 * HALO, patch_cols), jnp.float32),
            pltpu.VMEM((3 * BAND, BAND + 2 * HALO), jnp.bfloat16),
            pltpu.VMEM((3, patch_cols, patch_cols + 2 * EDGE), jnp.bfloat16),
            pltpu.VMEM((8, cols + 2 * EDGE), jnp.float32),
            pltpu.VMEM((2, LINES, cols), jnp.float32),
            pltpu.VMEM((blocks, LINES, block), jnp.bfloat16),
            pltpu.VMEM((blocks, depth, block), jnp.bfloat16),
            *[pltpu.SMEM(array.shape, array.dtype) for array in small],
            pltpu.SemaphoreType.DMA,
            pltpu.SemaphoreType.DMA((2,)),
            pltpu.SemaphoreType.DMA((5,)),
            pltpu.SemaphoreType.DMA((4, count, CHUNKS)),
            pltpu.SemaphoreType.DMA((count, CHUNKS)),
            pltpu.SemaphoreType.DMA((2, count)),
            pltpu.SemaphoreType.DMA((2, count)),
        ],
        compiler_params=pltpu.CompilerParams(
            collective_id=0, has_side_effects=True, vmem_limit_bytes=40 * 2**20
        ),
    )(*sources)
    result = pl.pallas_call(
        store_kernel,
        out_shape=jax.ShapeDtypeStruct((rows, cols), jnp.float32),
        in_specs=[vmem],
        out_specs=in_hbm,
        scratch_shapes=[pltpu.SemaphoreType.DMA((STORES,))],
        compiler_params=pltpu.CompilerParams(vmem_limit_bytes=2**20),
    )(value)
    return result[None]


def solution(mesh):
    placed = (
        P("tile", "ccd", None),
        P("tile", None, None, None),
        P("tile", None),
        P("ccd", "tile"),
        P(),
        P(),
        P(),
    )
    return jax.shard_map(
        on_device, mesh=mesh, in_specs=placed, out_specs=P("tile", "ccd", None), check_vma=False
    )
```

```python
import functools
import heapq

import jax
import jax.numpy as jnp
import ml_dtypes
import numpy as np
from jax import lax
from jax.experimental import pallas as pl
from jax.experimental.pallas import tpu as pltpu
from jax.sharding import PartitionSpec as P

HALF = 10
KSETS = 4
SIGMAS = (1.5, 3.0, 5.0)
HALO = 16
EDGE = 128
BAND = 128
MARGIN = 2
NOTHING = 3
CHUNKS = 4
LINES = 128


def basis_taps():
    positions = np.arange(-HALF, HALF + 1).astype(np.float64)
    kernels = []
    for sigma_value in SIGMAS:
        gauss = np.exp(-0.5 * (positions / sigma_value) ** 2)
        kernels.append(gauss / np.sum(gauss))
    return kernels


def smoothing_gains():
    near = [taps.astype(ml_dtypes.bfloat16).astype(np.float64) for taps in basis_taps()]
    return [1.0 / np.sum(taps) ** 2 for taps in near]


def banded(b, rows, cols, shift, first=0):
    shape = (rows, cols)
    distance = (
        lax.broadcasted_iota(jnp.int32, shape, 1)
        - lax.broadcasted_iota(jnp.int32, shape, 0)
        - (shift + first)
    )
    away = distance.astype(jnp.float32)
    taps = jnp.exp(away * away * (-0.5 / SIGMAS[b] ** 2)) * basis_taps()[b][HALF]
    return jnp.where(jnp.abs(away) <= HALF, taps, 0.0).astype(jnp.bfloat16)


def inner_size(count):
    best = 1
    for size in range(1, count + 1):
        if count % size == 0 and size * size <= count:
            best = size
    return best


def turns(d, qz, c, outer):
    late = c >= CHUNKS // 2
    ends = ((d == 0) & (qz == outer - 1)) | ((d == outer - 1) & (qz == 0))
    inside = (d > 0) & (d < outer - 1) & ((qz == d - 1) | (qz == d + 1))
    return (ends & late) | (inside & (late | (qz == 0) | (qz == outer - 1)))


def paths(me, q, c, count):
    inner = inner_size(count)
    outer = count // inner
    z, x = me // inner, me % inner
    qz, qx = q // inner, q % inner
    own = qx == x
    across = (qz == z) | (turns(z, qz, c, outer) ^ True)
    return (
        (z > 0) & (qz >= z) & (own | turns(z - 1, qz, c, outer)),
        (z < outer - 1) & (qz <= z) & (own | turns(z + 1, qz, c, outer)),
        across & (qx >= x) & (x > 0),
        across & (qx <= x) & (x < inner - 1),
    )


def place(c):
    return c + (c // 2) * (5 - 2 * c)


def programs(count):
    inner = inner_size(count)
    steps = (-inner, inner, -1, 1)
    free, order = {}, 0
    queue = [(0, False, me, me, c, me * CHUNKS + c) for me in range(count) for c in range(CHUNKS)]
    order = len(queue)
    heapq.heapify(queue)
    arrivals = [[] for _ in range(count)]
    drains = [[] for _ in range(count)]
    while queue:
        time, _, me, q, c, _ = heapq.heappop(queue)
        if q != me:
            arrivals[me].append((time, q * CHUNKS + c))
        sent = [time] if c % 2 == 0 else []
        for d, go in enumerate(paths(me, q, c, count)):
            if go:
                done = max(free.get((me, d), 0), time) + 1
                free[me, d] = done
                sent.append(done)
                to = me + steps[d]
                heapq.heappush(queue, (done, (q - to) % inner != 0, to, q, c, order))
                order += 1
        if sent:
            drains[me].append((max(sent) + MARGIN, q * CHUNKS + c))
    result = []
    for me in range(count):
        left = {q: CHUNKS for q in range(count)}
        steps = []
        for i, (time, event) in enumerate(arrivals[me]):
            left[event // CHUNKS] -= 1
            steps.append((time, 0, i, event * 4 + 2 * (left[event // CHUNKS] == 0)))
        for i, (time, event) in enumerate(drains[me]):
            steps.append((time, 1, i, event * 4 + 1))
        result.append([step[-1] for step in sorted(steps)])
    longest = max(len(steps) for steps in result)
    finals = [arrivals[me][-1][1] // CHUNKS for me in range(count)]
    return [steps + [NOTHING] * (longest - len(steps)) for steps in result], finals


def pick(me, values):
    value = jnp.int32(values[0])
    for i in range(1, len(values)):
        value = jnp.where(me == i, jnp.int32(values[i]), value)
    return value


def codes(count):
    digit, per_word = (128, 4) if count * CHUNKS * 4 <= 128 else (256, 3)
    steps, finals = programs(count)
    words = [
        [sum(v * digit**i for i, v in enumerate(line[first : first + per_word])) for line in steps]
        for first in range(0, len(steps[0]), per_word)
    ]
    return words, digit, per_word, len(steps[0]), finals


def spans(q, patch_cols, cols):
    first = pl.multiple_of(q * patch_cols, EDGE)
    left = pl.multiple_of(jnp.maximum(first - EDGE, 0), EDGE)
    right = pl.multiple_of(jnp.minimum(first + patch_cols, cols - EDGE), EDGE)
    return (
        (pl.ds(left, EDGE), slice(0, EDGE)),
        (pl.ds(first, patch_cols), slice(EDGE, EDGE + patch_cols)),
        (pl.ds(right, EDGE), slice(EDGE + patch_cols, 2 * EDGE + patch_cols)),
    )


def band_model(q, r, rows, strip, down, across, weights):
    patch_cols = strip.shape[2]
    first = pl.multiple_of(q * patch_cols, EDGE)
    wide = patch_cols + 2 * EDGE
    at = pl.multiple_of(r * BAND, BAND)
    pixel = strip[q, pl.ds(at, BAND + 2 * HALO), :].astype(jnp.bfloat16)
    tall = jnp.dot(down[...], pixel, preferred_element_type=jnp.float32)
    tall = tall.astype(jnp.bfloat16)
    v = (
        lax.broadcasted_iota(jnp.int32, (BAND, wide), 0) + r * BAND
    ).astype(jnp.float32) * (2.0 / rows) - (rows - 1) / rows
    model = None
    for b in range(3):
        flat = jnp.dot(
            tall[b * BAND : (b + 1) * BAND], across[b], preferred_element_type=jnp.float32
        )
        const = weights[b : b + 1, pl.ds(first, wide)]
        slope = weights[3 + b : 4 + b, pl.ds(first, wide)]
        term = (const + slope * v) * flat
        model = term if model is None else model + term
    return model


def strip_kernel(
    count, ccd_count, template, exposure, interp, offset_in, coef_in, index_in, cover_in,
    out, strip, down, across, weights, lines, pixels, mats, offsets, coef, index, cover,
    load_sem, line_sem, small_sem, send_sem, recv_sem, hsend_sem, hrecv_sem,
):
    me = lax.axis_index("tile")
    row = lax.axis_index("ccd")
    inner = inner_size(count)
    outer = count // inner
    z, x = me // inner, me % inner
    rows, patch_cols = template.shape
    cols = out.shape[1]
    part = rows // CHUNKS

    targets = (me - inner, me + inner, me - 1, me + 1)
    there = (z > 0, z < outer - 1, x > 0, x < inner - 1)
    halo_there = (row > 0, row < ccd_count - 1)

    barrier = pltpu.get_barrier_semaphore()
    total = jnp.int32(0)
    for target, exists in zip(targets, there):
        @pl.when(exists)
        def _():
            pl.semaphore_signal(barrier, inc=1, device_id=(row, target))
        total = total + exists.astype(jnp.int32)
    for step, exists in zip((-1, 1), halo_there):
        @pl.when(exists)
        def _():
            pl.semaphore_signal(barrier, inc=1, device_id=(row + step, me))
        total = total + exists.astype(jnp.int32)

    load = pltpu.make_async_copy(template, strip.at[me, pl.ds(HALO, rows)], load_sem)
    load.start()
    small = [
        pltpu.make_async_copy(source, target, small_sem.at[i])
        for i, (source, target) in enumerate(
            [(offset_in, offsets), (coef_in, coef), (index_in, index), (cover_in, cover), (interp, mats)]
        )
    ]
    for copy in small:
        copy.start()

    def line_copy(i, slot):
        return pltpu.make_async_copy(
            exposure.at[pl.ds(pl.multiple_of(i * LINES, LINES), LINES)], lines.at[slot], line_sem.at[slot]
        )

    line_copy(0, 0).start()
    pl.semaphore_wait(barrier, total)

    def send(q, c, d, own):
        first = place(c) * part
        piece = pl.ds(pl.multiple_of(HALO + first, HALO), part)
        return pltpu.make_async_remote_copy(
            src_ref=template.at[pl.ds(first, part)] if own else strip.at[q, piece],
            dst_ref=strip.at[q, piece],
            send_sem=send_sem.at[d, q, c],
            recv_sem=recv_sem.at[q, c],
            device_id=(row, targets[d]),
        )

    def halo(q, d):
        source = pl.ds(HALO, HALO) if d == 0 else pl.ds(rows, HALO)
        target = pl.ds(HALO + rows, HALO) if d == 0 else pl.ds(0, HALO)
        return pltpu.make_async_remote_copy(
            src_ref=strip.at[q, source],
            dst_ref=strip.at[q, target],
            send_sem=hsend_sem.at[d, q],
            recv_sem=hrecv_sem.at[d, q],
            device_id=(row + (-1 if d == 0 else 1), me),
        )

    for c in range(CHUNKS):
        for d in range(4):
            @pl.when(there[d])
            def _():
                send(me, c, d, True).start()
    load.wait()
    for d in range(2):
        @pl.when(halo_there[d])
        def _():
            halo(me, d).start()

    @pl.when(row == 0)
    def _():
        for q in range(count):
            strip[q, 0:HALO, :] = jnp.zeros((HALO, patch_cols), jnp.float32)

    @pl.when(row == ccd_count - 1)
    def _():
        for q in range(count):
            strip[q, rows + HALO : rows + 2 * HALO, :] = jnp.zeros((HALO, patch_cols), jnp.float32)

    for copy in small:
        copy.wait()

    blocks, depth, block = mats.shape

    def warp(i, carry):
        slot = i % 2
        line_copy(i, slot).wait()

        @pl.when(i + 1 < rows // LINES)
        def _():
            line_copy(i + 1, 1 - slot).start()

        for j in range(blocks):
            pixels[j] = lines[slot, :, j * block : (j + 1) * block].astype(jnp.bfloat16)
        here = pl.ds(pl.multiple_of(i * LINES, LINES), LINES)
        for j in range(blocks):
            start = offsets[0, j]
            window = [pixels[start + k] for k in range(depth // block)]
            value = jnp.dot(
                jnp.concatenate(window, axis=1), mats[j], preferred_element_type=jnp.float32
            )
            covered = cover[me, row, j * block // patch_cols]
            out[here, j * block : (j + 1) * block] = value * covered.astype(jnp.float32)
        return carry

    lax.fori_loop(0, rows // LINES, warp, 0)

    gains = smoothing_gains()
    u = (
        lax.broadcasted_iota(jnp.int32, (1, patch_cols), 1).astype(jnp.float32) * (2.0 / patch_cols)
        - (patch_cols - 1) / patch_cols
    )
    weights[...] = jnp.zeros(weights.shape, jnp.float32)
    for q in range(count):
        chosen = index[me, row, q]
        covered = cover[me, row, q].astype(jnp.float32)
        here = slice(EDGE + q * patch_cols, EDGE + (q + 1) * patch_cols)
        for b in range(3):
            terms = []
            for k in range(3):
                sets = [coef[b, k, i, me] for i in range(KSETS)]
                term = sets[0]
                for i in range(1, KSETS):
                    term = jnp.where(chosen == i, sets[i], term)
                terms.append(term * covered * float(gains[b]))
            const, slope, lift = terms
            weights[b : b + 1, here] = const + slope * u
            weights[3 + b : 4 + b, here] = jnp.full((1, patch_cols), lift, jnp.float32)

    def add_model(q):
        def band(r, carry):
            model = band_model(q, r, rows, strip, down, across, weights)
            here = pl.ds(pl.multiple_of(r * BAND, BAND), BAND)
            for there, piece in spans(q, patch_cols, cols):
                out[here, there] -= model[:, piece]
            return carry

        lax.fori_loop(0, rows // BAND, band, 0)

    def halos_in(q):
        for d in range(2):
            @pl.when(halo_there[1 - d])
            def _():
                halo(q, d).wait_recv()

    for b in range(3):
        down[b * BAND : (b + 1) * BAND, :] = banded(b, BAND, BAND + 2 * HALO, HALO)

        def fill(i, carry):
            first = pl.multiple_of(i * HALO, HALO)
            across[b, pl.ds(first, HALO), :] = banded(
                b, HALO, patch_cols + 2 * EDGE, EDGE, i * HALO
            )
            return carry

        lax.fori_loop(0, patch_cols // HALO, fill, 0)

    halos_in(me)
    add_model(me)

    table, digit, per_word, length, finals = codes(count)
    final = pick(me, finals)

    def step(_, words):
        words = list(words)
        code = words[0] % digit
        for w in range(len(words)):
            words[w] = words[w] // digit
            if w + 1 < len(words):
                words[w] = words[w] + (words[w + 1] % digit) * digit ** (per_word - 1)
        kind, event = code % 4, code // 4
        q, c = event // CHUNKS, event % CHUNKS
        onward = paths(me, q, c, count)
        halos = [(c == 2 * d) & halo_there[d] for d in range(2)]

        @pl.when(kind % 2 == 0)
        def _():
            send(q, c, 0, False).wait_recv()
            for d in range(4):
                @pl.when(onward[d])
                def _():
                    send(q, c, d, False).start()
            for d in range(2):
                @pl.when(halos[d])
                def _():
                    halo(q, d).start()

        @pl.when(kind == 2)
        def _():
            halos_in(q)

            @pl.when(q != final)
            def _():
                add_model(q)

        @pl.when(kind == 1)
        def _():
            for d in range(4):
                @pl.when(onward[d])
                def _():
                    send(q, c, d, False).wait_send()
            for d in range(2):
                @pl.when(halos[d])
                def _():
                    halo(q, d).wait_send()

        return tuple(words)

    lax.fori_loop(0, length, step, tuple(pick(me, line) for line in table))


def finish_kernel(count, strip, down, across, weights, value, out, work, far_sem, near_sem):
    rows, cols = value.shape
    patch_cols = strip.shape[2]
    final = pick(lax.axis_index("tile"), codes(count)[-1])
    pieces = spans(final, patch_cols, cols)
    within = (final > 0, final >= 0, final < count - 1)

    def far(q, shift, size):
        here = (slice(None), pl.ds(q * patch_cols + shift, size))
        return pltpu.make_async_copy(value.at[here], out.at[here], far_sem.at[q])

    def near(i, r):
        there, piece = pieces[i]
        return pltpu.make_async_copy(
            work.at[pl.ds(r * BAND, BAND), piece], out.at[pl.ds(r * BAND, BAND), there], near_sem.at[i, r]
        )

    def far_copies(act):
        for q in range(count):
            @pl.when((q < final - 1) | (q > final + 1))
            def _():
                act(far(q, 0, patch_cols))

            @pl.when(q == final - 1)
            def _():
                act(far(q, 0, patch_cols - EDGE))

            @pl.when(q == final + 1)
            def _():
                act(far(q, EDGE, patch_cols - EDGE))

    far_copies(lambda copy: copy.start())
    for r in range(rows // BAND):
        model = band_model(final, r, rows, strip, down, across, weights)
        here = pl.ds(r * BAND, BAND)
        for i, (there, piece) in enumerate(pieces):
            work[here, piece] = value[here, there] - model[:, piece]

            @pl.when(within[i])
            def _():
                near(i, r).start()
    far_copies(lambda copy: copy.wait())
    for r in range(rows // BAND):
        for i in range(3):
            @pl.when(within[i])
            def _():
                near(i, r).wait()


def on_device(exposures, interp, col_offsets, template, coef_table, coef_index, intersection):
    rows, cols = exposures.shape[1:]
    patch_cols = template.shape[1]
    count, ccd_count = lax.axis_size("tile"), lax.axis_size("ccd")
    blocks, depth, block = interp.shape[1:]
    small = [col_offsets, coef_table.transpose(2, 3, 1, 0), coef_index, intersection]

    sources = [
        pltpu.with_memory_space_constraint(array, pltpu.HBM)
        for array in (template, exposures[0], interp[0], *small)
    ]
    in_hbm = pl.BlockSpec(memory_space=pltpu.HBM)
    vmem = pl.BlockSpec(memory_space=pltpu.VMEM)
    shapes = [
        ((rows, cols), jnp.float32),
        ((count, rows + 2 * HALO, patch_cols), jnp.float32),
        ((3 * BAND, BAND + 2 * HALO), jnp.bfloat16),
        ((3, patch_cols, patch_cols + 2 * EDGE), jnp.bfloat16),
        ((8, cols + 2 * EDGE), jnp.float32),
    ]
    value, strip, down, across, weights = pl.pallas_call(
        functools.partial(strip_kernel, count, ccd_count),
        out_shape=[jax.ShapeDtypeStruct(*shape) for shape in shapes],
        in_specs=[in_hbm] * 7,
        out_specs=[vmem] * 5,
        scratch_shapes=[
            pltpu.VMEM((2, LINES, cols), jnp.float32),
            pltpu.VMEM((blocks, LINES, block), jnp.bfloat16),
            pltpu.VMEM((blocks, depth, block), jnp.bfloat16),
            *[pltpu.SMEM(array.shape, array.dtype) for array in small],
            pltpu.SemaphoreType.DMA,
            pltpu.SemaphoreType.DMA((2,)),
            pltpu.SemaphoreType.DMA((5,)),
            pltpu.SemaphoreType.DMA((4, count, CHUNKS)),
            pltpu.SemaphoreType.DMA((count, CHUNKS)),
            pltpu.SemaphoreType.DMA((2, count)),
            pltpu.SemaphoreType.DMA((2, count)),
        ],
        compiler_params=pltpu.CompilerParams(
            collective_id=0, has_side_effects=True, vmem_limit_bytes=16 * 2**20
        ),
    )(*sources)
    result = pl.pallas_call(
        functools.partial(finish_kernel, count),
        out_shape=jax.ShapeDtypeStruct((rows, cols), jnp.float32),
        in_specs=[vmem] * 5,
        out_specs=in_hbm,
        scratch_shapes=[
            pltpu.VMEM((rows, patch_cols + 2 * EDGE), jnp.float32),
            pltpu.SemaphoreType.DMA((count,)),
            pltpu.SemaphoreType.DMA((3, rows // BAND)),
        ],
        compiler_params=pltpu.CompilerParams(vmem_limit_bytes=16 * 2**20),
    )(strip, down, across, weights, value)
    return result[None]


def solution(mesh):
    placed = (
        P("tile", "ccd", None),
        P("tile", None, None, None),
        P("tile", None),
        P("ccd", "tile"),
        P(),
        P(),
        P(),
    )
    return jax.shard_map(
        on_device, mesh=mesh, in_specs=placed, out_specs=P("tile", "ccd", None), check_vma=False
    )
```

```python
import functools
import heapq

import jax
import jax.numpy as jnp
import ml_dtypes
import numpy as np
from jax import lax
from jax.experimental import pallas as pl
from jax.experimental.pallas import tpu as pltpu
from jax.sharding import PartitionSpec as P

HALF = 10
KSETS = 4
SIGMAS = (1.5, 3.0, 5.0)
HALO = 16
EDGE = 128
BAND = 128
MARGIN = 1
NOTHING = 3
CHUNKS = 4
LINES = 128


def basis_taps():
    positions = np.arange(-HALF, HALF + 1).astype(np.float64)
    kernels = []
    for sigma_value in SIGMAS:
        gauss = np.exp(-0.5 * (positions / sigma_value) ** 2)
        kernels.append(gauss / np.sum(gauss))
    return kernels


def smoothing_gains():
    near = [taps.astype(ml_dtypes.bfloat16).astype(np.float64) for taps in basis_taps()]
    return [1.0 / np.sum(taps) ** 2 for taps in near]


def banded(b, rows, cols, shift, first=0):
    shape = (rows, cols)
    distance = (
        lax.broadcasted_iota(jnp.int32, shape, 1)
        - lax.broadcasted_iota(jnp.int32, shape, 0)
        - (shift + first)
    )
    away = distance.astype(jnp.float32)
    taps = jnp.exp(away * away * (-0.5 / SIGMAS[b] ** 2)) * basis_taps()[b][HALF]
    return jnp.where(jnp.abs(away) <= HALF, taps, 0.0).astype(jnp.bfloat16)


def inner_size(count):
    best = 1
    for size in range(1, count + 1):
        if count % size == 0 and size * size <= count:
            best = size
    return best


def turns(d, qz, c, outer):
    late = c >= CHUNKS // 2
    ends = ((d == 0) & (qz == outer - 1)) | ((d == outer - 1) & (qz == 0))
    inside = (d > 0) & (d < outer - 1) & ((qz == d - 1) | (qz == d + 1))
    return (ends & late) | (inside & (late | (qz == 0) | (qz == outer - 1)))


def paths(me, q, c, count):
    inner = inner_size(count)
    outer = count // inner
    z, x = me // inner, me % inner
    qz, qx = q // inner, q % inner
    own = qx == x
    across = (qz == z) | (turns(z, qz, c, outer) ^ True)
    return (
        (z > 0) & (qz >= z) & (own | turns(z - 1, qz, c, outer)),
        (z < outer - 1) & (qz <= z) & (own | turns(z + 1, qz, c, outer)),
        across & (qx >= x) & (x > 0),
        across & (qx <= x) & (x < inner - 1),
    )


def place(c):
    half = CHUNKS // 2
    return c + (c // half) * (CHUNKS + half - 1 - 2 * c)


def programs(count):
    inner = inner_size(count)
    steps = (-inner, inner, -1, 1)
    free, order = {}, 0
    queue = [(0, False, me, me, c, me * CHUNKS + c) for me in range(count) for c in range(CHUNKS)]
    order = len(queue)
    heapq.heapify(queue)
    arrivals = [[] for _ in range(count)]
    drains = [[] for _ in range(count)]
    while queue:
        time, _, me, q, c, _ = heapq.heappop(queue)
        if q != me:
            arrivals[me].append((time, q * CHUNKS + c))
        sent = [time] if c % (CHUNKS // 2) == 0 else []
        for d, go in enumerate(paths(me, q, c, count)):
            if go:
                done = max(free.get((me, d), 0), time) + 1
                free[me, d] = done
                sent.append(done)
                to = me + steps[d]
                heapq.heappush(queue, (done, (q - to) % inner != 0, to, q, c, order))
                order += 1
        if sent:
            drains[me].append((max(sent) + MARGIN, q * CHUNKS + c))
    result = []
    for me in range(count):
        left = {q: CHUNKS for q in range(count)}
        steps = []
        for i, (time, event) in enumerate(arrivals[me]):
            left[event // CHUNKS] -= 1
            steps.append((time, 0, i, event * 4 + 2 * (left[event // CHUNKS] == 0)))
        for i, (time, event) in enumerate(drains[me]):
            steps.append((time, 1, i, event * 4 + 1))
        result.append([step[-1] for step in sorted(steps)])
    longest = max(len(steps) for steps in result)
    finals = [arrivals[me][-1][1] // CHUNKS for me in range(count)]
    return [[NOTHING] * (longest - len(steps)) + steps for steps in result], finals


def pick(me, values):
    value = jnp.int32(values[0])
    for i in range(1, len(values)):
        value = jnp.where(me == i, jnp.int32(values[i]), value)
    return value


def codes(count):
    bits = (count * CHUNKS * 4 - 1).bit_length()
    digit, per_word = 2**bits, 30 // bits
    steps, finals = programs(count)
    words = [
        [sum(v * digit**i for i, v in enumerate(line[first : first + per_word])) for line in steps]
        for first in range(0, len(steps[0]), per_word)
    ]
    return words, digit, per_word, len(steps[0]), finals


def spans(q, patch_cols, cols):
    first = pl.multiple_of(q * patch_cols, EDGE)
    left = pl.multiple_of(jnp.maximum(first - EDGE, 0), EDGE)
    right = pl.multiple_of(jnp.minimum(first + patch_cols, cols - EDGE), EDGE)
    return (
        (pl.ds(left, EDGE), slice(0, EDGE)),
        (pl.ds(first, patch_cols), slice(EDGE, EDGE + patch_cols)),
        (pl.ds(right, EDGE), slice(EDGE + patch_cols, 2 * EDGE + patch_cols)),
    )


def band_model(q, r, rows, strip, down, across, weights):
    patch_cols = strip.shape[2]
    first = pl.multiple_of(q * patch_cols, EDGE)
    wide = patch_cols + 2 * EDGE
    at = pl.multiple_of(r * BAND, BAND)
    pixel = strip[q, pl.ds(at, BAND + 2 * HALO), :].astype(jnp.bfloat16)
    tall = jnp.dot(down[...], pixel, preferred_element_type=jnp.float32)
    tall = tall.astype(jnp.bfloat16)
    v = (
        lax.broadcasted_iota(jnp.int32, (BAND, wide), 0) + r * BAND
    ).astype(jnp.float32) * (2.0 / rows) - (rows - 1) / rows
    model = None
    for b in range(3):
        flat = jnp.dot(
            tall[b * BAND : (b + 1) * BAND], across[b], preferred_element_type=jnp.float32
        )
        const = weights[b : b + 1, pl.ds(first, wide)]
        slope = weights[3 + b : 4 + b, pl.ds(first, wide)]
        term = (const + slope * v) * flat
        model = term if model is None else model + term
    return model


def strip_kernel(
    count, ccd_count, template, exposure, interp, offset_in, coef_in, index_in, cover_in,
    out, strip, down, across, weights, lines, pixels, mats, offsets, coef, index, cover,
    load_sem, line_sem, small_sem, send_sem, recv_sem, hsend_sem, hrecv_sem,
):
    me = lax.axis_index("tile")
    row = lax.axis_index("ccd")
    inner = inner_size(count)
    outer = count // inner
    z, x = me // inner, me % inner
    rows, patch_cols = template.shape
    cols = out.shape[1]
    part = rows // CHUNKS

    targets = (me - inner, me + inner, me - 1, me + 1)
    there = (z > 0, z < outer - 1, x > 0, x < inner - 1)
    halo_there = (row > 0, row < ccd_count - 1)

    barrier = pltpu.get_barrier_semaphore()
    total = jnp.int32(0)
    for target, exists in zip(targets, there):
        @pl.when(exists)
        def _():
            pl.semaphore_signal(barrier, inc=1, device_id=(row, target))
        total = total + exists.astype(jnp.int32)
    for step, exists in zip((-1, 1), halo_there):
        @pl.when(exists)
        def _():
            pl.semaphore_signal(barrier, inc=1, device_id=(row + step, me))
        total = total + exists.astype(jnp.int32)

    pl.semaphore_wait(barrier, total)

    def send(q, c, d, own):
        first = place(c) * part
        piece = pl.ds(pl.multiple_of(HALO + first, HALO), part)
        return pltpu.make_async_remote_copy(
            src_ref=template.at[pl.ds(first, part)] if own else strip.at[q, piece],
            dst_ref=strip.at[q, piece],
            send_sem=send_sem.at[d, q, c],
            recv_sem=recv_sem.at[q, c],
            device_id=(row, targets[d]),
        )

    def halo(q, d):
        source = pl.ds(HALO, HALO) if d == 0 else pl.ds(rows, HALO)
        target = pl.ds(HALO + rows, HALO) if d == 0 else pl.ds(0, HALO)
        return pltpu.make_async_remote_copy(
            src_ref=strip.at[q, source],
            dst_ref=strip.at[q, target],
            send_sem=hsend_sem.at[d, q],
            recv_sem=hrecv_sem.at[d, q],
            device_id=(row + (-1 if d == 0 else 1), me),
        )

    for c in range(CHUNKS):
        for d in range(4):
            @pl.when(there[d])
            def _():
                send(me, c, d, True).start()
    load = pltpu.make_async_copy(template, strip.at[me, pl.ds(HALO, rows)], load_sem)
    load.start()
    small = [
        pltpu.make_async_copy(source, target, small_sem.at[i])
        for i, (source, target) in enumerate(
            [(offset_in, offsets), (coef_in, coef), (index_in, index), (cover_in, cover), (interp, mats)]
        )
    ]
    for copy in small:
        copy.start()

    def line_copy(i, slot):
        return pltpu.make_async_copy(
            exposure.at[pl.ds(pl.multiple_of(i * LINES, LINES), LINES)], lines.at[slot], line_sem.at[slot]
        )

    line_copy(0, 0).start()
    load.wait()
    for d in range(2):
        @pl.when(halo_there[d])
        def _():
            halo(me, d).start()

    @pl.when(row == 0)
    def _():
        for q in range(count):
            strip[q, 0:HALO, :] = jnp.zeros((HALO, patch_cols), jnp.float32)

    @pl.when(row == ccd_count - 1)
    def _():
        for q in range(count):
            strip[q, rows + HALO : rows + 2 * HALO, :] = jnp.zeros((HALO, patch_cols), jnp.float32)

    for copy in small:
        copy.wait()

    blocks, depth, block = mats.shape

    def warp(i, carry):
        slot = i % 2
        line_copy(i, slot).wait()

        @pl.when(i + 1 < rows // LINES)
        def _():
            line_copy(i + 1, 1 - slot).start()

        for j in range(blocks):
            pixels[j] = lines[slot, :, j * block : (j + 1) * block].astype(jnp.bfloat16)
        here = pl.ds(pl.multiple_of(i * LINES, LINES), LINES)
        for j in range(blocks):
            start = offsets[0, j]
            window = [pixels[start + k] for k in range(depth // block)]
            value = jnp.dot(
                jnp.concatenate(window, axis=1), mats[j], preferred_element_type=jnp.float32
            )
            covered = cover[me, row, j * block // patch_cols]
            out[here, j * block : (j + 1) * block] = value * covered.astype(jnp.float32)
        return carry

    lax.fori_loop(0, rows // LINES, warp, 0)

    gains = smoothing_gains()
    u = (
        lax.broadcasted_iota(jnp.int32, (1, patch_cols), 1).astype(jnp.float32) * (2.0 / patch_cols)
        - (patch_cols - 1) / patch_cols
    )
    weights[...] = jnp.zeros(weights.shape, jnp.float32)
    for q in range(count):
        chosen = index[me, row, q]
        covered = cover[me, row, q].astype(jnp.float32)
        here = slice(EDGE + q * patch_cols, EDGE + (q + 1) * patch_cols)
        for b in range(3):
            terms = []
            for k in range(3):
                sets = [coef[b, k, i, me] for i in range(KSETS)]
                term = sets[0]
                for i in range(1, KSETS):
                    term = jnp.where(chosen == i, sets[i], term)
                terms.append(term * covered * float(gains[b]))
            const, slope, lift = terms
            weights[b : b + 1, here] = const + slope * u
            weights[3 + b : 4 + b, here] = jnp.full((1, patch_cols), lift, jnp.float32)

    def add_model(q):
        def band(r, carry):
            model = band_model(q, r, rows, strip, down, across, weights)
            here = pl.ds(pl.multiple_of(r * BAND, BAND), BAND)
            for there, piece in spans(q, patch_cols, cols):
                out[here, there] -= model[:, piece]
            return carry

        lax.fori_loop(0, rows // BAND, band, 0)

    def halos_in(q):
        for d in range(2):
            @pl.when(halo_there[1 - d])
            def _():
                halo(q, d).wait_recv()

    for b in range(3):
        down[b * BAND : (b + 1) * BAND, :] = banded(b, BAND, BAND + 2 * HALO, HALO)

        def fill(i, carry):
            first = pl.multiple_of(i * HALO, HALO)
            across[b, pl.ds(first, HALO), :] = banded(
                b, HALO, patch_cols + 2 * EDGE, EDGE, i * HALO
            )
            return carry

        lax.fori_loop(0, patch_cols // HALO, fill, 0)

    halos_in(me)
    add_model(me)

    table, digit, per_word, length, finals = codes(count)
    final = pick(me, finals)

    def step(_, words):
        words = list(words)
        code = words[0] % digit
        for w in range(len(words)):
            words[w] = words[w] // digit
            if w + 1 < len(words):
                words[w] = words[w] + (words[w + 1] % digit) * digit ** (per_word - 1)
        kind, event = code % 4, code // 4
        q, c = event // CHUNKS, event % CHUNKS
        onward = paths(me, q, c, count)
        halos = [(c == CHUNKS // 2 * d) & halo_there[d] for d in range(2)]

        @pl.when(kind % 2 == 0)
        def _():
            send(q, c, 0, False).wait_recv()
            for d in range(2):
                @pl.when(halos[d])
                def _():
                    halo(q, d).start()
            for d in range(4):
                @pl.when(onward[d])
                def _():
                    send(q, c, d, False).start()

        @pl.when(kind == 2)
        def _():
            halos_in(q)

            @pl.when(q != final)
            def _():
                add_model(q)

        @pl.when(kind == 1)
        def _():
            for d in range(4):
                @pl.when(onward[d])
                def _():
                    send(q, c, d, False).wait_send()
            for d in range(2):
                @pl.when(halos[d])
                def _():
                    halo(q, d).wait_send()

        return tuple(words)

    lax.fori_loop(0, length, step, tuple(pick(me, line) for line in table))


def finish_kernel(count, strip, down, across, weights, value, out, work, far_sem, near_sem):
    rows, cols = value.shape
    patch_cols = strip.shape[2]
    final = pick(lax.axis_index("tile"), codes(count)[-1])
    pieces = spans(final, patch_cols, cols)
    within = (final > 0, final >= 0, final < count - 1)

    def far(q, shift, size):
        here = (slice(None), pl.ds(q * patch_cols + shift, size))
        return pltpu.make_async_copy(value.at[here], out.at[here], far_sem.at[q])

    def near(i, r):
        there, piece = pieces[i]
        return pltpu.make_async_copy(
            work.at[pl.ds(r * BAND, BAND), piece], out.at[pl.ds(r * BAND, BAND), there], near_sem.at[i, r]
        )

    def far_copies(act):
        for q in range(count):
            @pl.when((q < final - 1) | (q > final + 1))
            def _():
                act(far(q, 0, patch_cols))

            @pl.when(q == final - 1)
            def _():
                act(far(q, 0, patch_cols - EDGE))

            @pl.when(q == final + 1)
            def _():
                act(far(q, EDGE, patch_cols - EDGE))

    far_copies(lambda copy: copy.start())
    for r in range(rows // BAND):
        model = band_model(final, r, rows, strip, down, across, weights)
        here = pl.ds(r * BAND, BAND)
        for i, (there, piece) in enumerate(pieces):
            work[here, piece] = value[here, there] - model[:, piece]

            @pl.when(within[i])
            def _():
                near(i, r).start()
    far_copies(lambda copy: copy.wait())
    for r in range(rows // BAND):
        for i in range(3):
            @pl.when(within[i])
            def _():
                near(i, r).wait()


def on_device(exposures, interp, col_offsets, template, coef_table, coef_index, intersection):
    rows, cols = exposures.shape[1:]
    patch_cols = template.shape[1]
    count, ccd_count = lax.axis_size("tile"), lax.axis_size("ccd")
    blocks, depth, block = interp.shape[1:]
    small = [col_offsets, coef_table.transpose(2, 3, 1, 0), coef_index, intersection]

    sources = [
        pltpu.with_memory_space_constraint(array, pltpu.HBM)
        for array in (template, exposures[0], interp[0], *small)
    ]
    in_hbm = pl.BlockSpec(memory_space=pltpu.HBM)
    vmem = pl.BlockSpec(memory_space=pltpu.VMEM)
    shapes = [
        ((rows, cols), jnp.float32),
        ((count, rows + 2 * HALO, patch_cols), jnp.float32),
        ((3 * BAND, BAND + 2 * HALO), jnp.bfloat16),
        ((3, patch_cols, patch_cols + 2 * EDGE), jnp.bfloat16),
        ((8, cols + 2 * EDGE), jnp.float32),
    ]
    value, strip, down, across, weights = pl.pallas_call(
        functools.partial(strip_kernel, count, ccd_count),
        out_shape=[jax.ShapeDtypeStruct(*shape) for shape in shapes],
        in_specs=[in_hbm] * 7,
        out_specs=[vmem] * 5,
        scratch_shapes=[
            pltpu.VMEM((2, LINES, cols), jnp.float32),
            pltpu.VMEM((blocks, LINES, block), jnp.bfloat16),
            pltpu.VMEM((blocks, depth, block), jnp.bfloat16),
            *[pltpu.SMEM(array.shape, array.dtype) for array in small],
            pltpu.SemaphoreType.DMA,
            pltpu.SemaphoreType.DMA((2,)),
            pltpu.SemaphoreType.DMA((5,)),
            pltpu.SemaphoreType.DMA((4, count, CHUNKS)),
            pltpu.SemaphoreType.DMA((count, CHUNKS)),
            pltpu.SemaphoreType.DMA((2, count)),
            pltpu.SemaphoreType.DMA((2, count)),
        ],
        compiler_params=pltpu.CompilerParams(
            collective_id=0, has_side_effects=True, vmem_limit_bytes=16 * 2**20
        ),
    )(*sources)
    result = pl.pallas_call(
        functools.partial(finish_kernel, count),
        out_shape=jax.ShapeDtypeStruct((rows, cols), jnp.float32),
        in_specs=[vmem] * 5,
        out_specs=in_hbm,
        scratch_shapes=[
            pltpu.VMEM((rows, patch_cols + 2 * EDGE), jnp.float32),
            pltpu.SemaphoreType.DMA((count,)),
            pltpu.SemaphoreType.DMA((3, rows // BAND)),
        ],
        compiler_params=pltpu.CompilerParams(vmem_limit_bytes=16 * 2**20),
    )(strip, down, across, weights, value)
    return result[None]


def solution(mesh):
    placed = (
        P("tile", "ccd", None),
        P("tile", None, None, None),
        P("tile", None),
        P("ccd", "tile"),
        P(),
        P(),
        P(),
    )
    return jax.shard_map(
        on_device, mesh=mesh, in_specs=placed, out_specs=P("tile", "ccd", None), check_vma=False
    )
```

```python
import functools
import heapq

import jax
import jax.numpy as jnp
import ml_dtypes
import numpy as np
from jax import lax
from jax.experimental import pallas as pl
from jax.experimental.pallas import tpu as pltpu
from jax.sharding import PartitionSpec as P

HALF = 10
KSETS = 4
SIGMAS = (1.5, 3.0, 5.0)
HALO = 16
EDGE = 128
BAND = 128
MARGIN = 1
NOTHING = 3
CHUNKS = 4
LINES = 128


def basis_taps():
    positions = np.arange(-HALF, HALF + 1).astype(np.float64)
    kernels = []
    for sigma_value in SIGMAS:
        gauss = np.exp(-0.5 * (positions / sigma_value) ** 2)
        kernels.append(gauss / np.sum(gauss))
    return kernels


def smoothing_gains():
    near = [taps.astype(ml_dtypes.bfloat16).astype(np.float64) for taps in basis_taps()]
    return [1.0 / np.sum(taps) ** 2 for taps in near]


def banded(b, rows, cols, shift, first=0):
    shape = (rows, cols)
    distance = (
        lax.broadcasted_iota(jnp.int32, shape, 1)
        - lax.broadcasted_iota(jnp.int32, shape, 0)
        - (shift + first)
    )
    away = distance.astype(jnp.float32)
    taps = jnp.exp(away * away * (-0.5 / SIGMAS[b] ** 2)) * basis_taps()[b][HALF]
    return jnp.where(jnp.abs(away) <= HALF, taps, 0.0).astype(jnp.bfloat16)


def inner_size(count):
    best = 1
    for size in range(1, count + 1):
        if count % size == 0 and size * size <= count:
            best = size
    return best


def turns(d, qz, c, outer):
    late = c >= CHUNKS // 2
    ends = ((d == 0) & (qz == outer - 1)) | ((d == outer - 1) & (qz == 0))
    inside = (d > 0) & (d < outer - 1) & ((qz == d - 1) | (qz == d + 1))
    return (ends & late) | (inside & (late | (qz == 0) | (qz == outer - 1)))


def paths(me, q, c, count):
    inner = inner_size(count)
    outer = count // inner
    z, x = me // inner, me % inner
    qz, qx = q // inner, q % inner
    own = qx == x
    across = (qz == z) | (turns(z, qz, c, outer) ^ True)
    return (
        (z > 0) & (qz >= z) & (own | turns(z - 1, qz, c, outer)),
        (z < outer - 1) & (qz <= z) & (own | turns(z + 1, qz, c, outer)),
        across & (qx >= x) & (x > 0),
        across & (qx <= x) & (x < inner - 1),
    )


def place(c):
    half = CHUNKS // 2
    return c + (c // half) * (CHUNKS + half - 1 - 2 * c)


def programs(count):
    inner = inner_size(count)
    steps = (-inner, inner, -1, 1)
    free, order = {}, 0
    queue = [(0, False, me, me, c, me * CHUNKS + c) for me in range(count) for c in range(CHUNKS)]
    order = len(queue)
    heapq.heapify(queue)
    arrivals = [[] for _ in range(count)]
    drains = [[] for _ in range(count)]
    while queue:
        time, _, me, q, c, _ = heapq.heappop(queue)
        if q != me:
            arrivals[me].append((time, q * CHUNKS + c))
        sent = [time] if c % (CHUNKS // 2) == 0 else []
        for d, go in enumerate(paths(me, q, c, count)):
            if go:
                done = max(free.get((me, d), 0), time) + 1
                free[me, d] = done
                sent.append(done)
                to = me + steps[d]
                heapq.heappush(queue, (done, (q - to) % inner != 0, to, q, c, order))
                order += 1
        if sent:
            drains[me].append((max(sent) + MARGIN, q * CHUNKS + c))
    result = []
    for me in range(count):
        left = {q: CHUNKS for q in range(count)}
        steps = []
        for i, (time, event) in enumerate(arrivals[me]):
            left[event // CHUNKS] -= 1
            steps.append((time, 0, i, event * 4 + 2 * (left[event // CHUNKS] == 0)))
        for i, (time, event) in enumerate(drains[me]):
            steps.append((time, 1, i, event * 4 + 1))
        result.append([step[-1] for step in sorted(steps)])
    longest = max(len(steps) for steps in result)
    finals = [arrivals[me][-1][1] // CHUNKS for me in range(count)]
    return [[NOTHING] * (longest - len(steps)) + steps for steps in result], finals


def pick(me, values):
    value = jnp.int32(values[0])
    for i in range(1, len(values)):
        value = jnp.where(me == i, jnp.int32(values[i]), value)
    return value


def codes(count):
    bits = (count * CHUNKS * 4 - 1).bit_length()
    digit, per_word = 2**bits, 30 // bits
    steps, finals = programs(count)
    words = [
        [sum(v * digit**i for i, v in enumerate(line[first : first + per_word])) for line in steps]
        for first in range(0, len(steps[0]), per_word)
    ]
    return words, digit, per_word, len(steps[0]), finals


def spans(q, patch_cols, cols):
    first = pl.multiple_of(q * patch_cols, EDGE)
    left = pl.multiple_of(jnp.maximum(first - EDGE, 0), EDGE)
    right = pl.multiple_of(jnp.minimum(first + patch_cols, cols - EDGE), EDGE)
    return (
        (pl.ds(left, EDGE), slice(0, EDGE)),
        (pl.ds(first, patch_cols), slice(EDGE, EDGE + patch_cols)),
        (pl.ds(right, EDGE), slice(EDGE + patch_cols, 2 * EDGE + patch_cols)),
    )


def band_model(q, r, rows, strip, down, across, weights):
    patch_cols = strip.shape[2]
    first = pl.multiple_of(q * patch_cols, EDGE)
    wide = patch_cols + 2 * EDGE
    at = pl.multiple_of(r * BAND, BAND)
    pixel = strip[q, pl.ds(at, BAND + 2 * HALO), :].astype(jnp.bfloat16)
    tall = jnp.dot(down[...], pixel, preferred_element_type=jnp.float32)
    tall = tall.astype(jnp.bfloat16)
    v = (
        lax.broadcasted_iota(jnp.int32, (BAND, wide), 0) + r * BAND
    ).astype(jnp.float32) * (2.0 / rows) - (rows - 1) / rows
    model = None
    for b in range(3):
        flat = jnp.dot(
            tall[b * BAND : (b + 1) * BAND], across[b], preferred_element_type=jnp.float32
        )
        const = weights[b : b + 1, pl.ds(first, wide)]
        slope = weights[3 + b : 4 + b, pl.ds(first, wide)]
        term = (const + slope * v) * flat
        model = term if model is None else model + term
    return model


def strip_kernel(
    count, ccd_count, template, exposure, interp, offset_in, coef_in, index_in, cover_in,
    out, strip, down, across, weights, lines, pixels, mats, offsets, coef, index, cover,
    load_sem, line_sem, small_sem, send_sem, recv_sem, hsend_sem, hrecv_sem,
):
    me = lax.axis_index("tile")
    row = lax.axis_index("ccd")
    inner = inner_size(count)
    outer = count // inner
    z, x = me // inner, me % inner
    rows, patch_cols = template.shape
    cols = out.shape[1]
    part = rows // CHUNKS

    targets = (me - inner, me + inner, me - 1, me + 1)
    there = (z > 0, z < outer - 1, x > 0, x < inner - 1)
    halo_there = (row > 0, row < ccd_count - 1)

    load = pltpu.make_async_copy(template, strip.at[me, pl.ds(HALO, rows)], load_sem)
    load.start()

    barrier = pltpu.get_barrier_semaphore()
    total = jnp.int32(0)
    for target, exists in zip(targets, there):
        @pl.when(exists)
        def _():
            pl.semaphore_signal(barrier, inc=1, device_id=(row, target))
        total = total + exists.astype(jnp.int32)
    for step, exists in zip((-1, 1), halo_there):
        @pl.when(exists)
        def _():
            pl.semaphore_signal(barrier, inc=1, device_id=(row + step, me))
        total = total + exists.astype(jnp.int32)

    load.wait()
    pl.semaphore_wait(barrier, total)

    def send(q, c, d):
        first = place(c) * part
        piece = pl.ds(pl.multiple_of(HALO + first, HALO), part)
        return pltpu.make_async_remote_copy(
            src_ref=strip.at[q, piece],
            dst_ref=strip.at[q, piece],
            send_sem=send_sem.at[d, q, c],
            recv_sem=recv_sem.at[q, c],
            device_id=(row, targets[d]),
        )

    def halo(q, d):
        source = pl.ds(HALO, HALO) if d == 0 else pl.ds(rows, HALO)
        target = pl.ds(HALO + rows, HALO) if d == 0 else pl.ds(0, HALO)
        return pltpu.make_async_remote_copy(
            src_ref=strip.at[q, source],
            dst_ref=strip.at[q, target],
            send_sem=hsend_sem.at[d, q],
            recv_sem=hrecv_sem.at[d, q],
            device_id=(row + (-1 if d == 0 else 1), me),
        )

    for c in range(CHUNKS):
        for d in (2, 3, 0, 1):
            @pl.when(there[d])
            def _():
                send(me, c, d).start()
    small = [
        pltpu.make_async_copy(source, target, small_sem.at[i])
        for i, (source, target) in enumerate(
            [(offset_in, offsets), (coef_in, coef), (index_in, index), (cover_in, cover), (interp, mats)]
        )
    ]
    for copy in small:
        copy.start()

    def line_copy(i, slot):
        return pltpu.make_async_copy(
            exposure.at[pl.ds(pl.multiple_of(i * LINES, LINES), LINES)], lines.at[slot], line_sem.at[slot]
        )

    line_copy(0, 0).start()
    for d in range(2):
        @pl.when(halo_there[d])
        def _():
            halo(me, d).start()

    @pl.when(row == 0)
    def _():
        for q in range(count):
            strip[q, 0:HALO, :] = jnp.zeros((HALO, patch_cols), jnp.float32)

    @pl.when(row == ccd_count - 1)
    def _():
        for q in range(count):
            strip[q, rows + HALO : rows + 2 * HALO, :] = jnp.zeros((HALO, patch_cols), jnp.float32)

    for copy in small:
        copy.wait()

    blocks, depth, block = mats.shape

    def warp(i, carry):
        slot = i % 2
        line_copy(i, slot).wait()

        @pl.when(i + 1 < rows // LINES)
        def _():
            line_copy(i + 1, 1 - slot).start()

        for j in range(blocks):
            pixels[j] = lines[slot, :, j * block : (j + 1) * block].astype(jnp.bfloat16)
        here = pl.ds(pl.multiple_of(i * LINES, LINES), LINES)
        for j in range(blocks):
            start = offsets[0, j]
            window = [pixels[start + k] for k in range(depth // block)]
            value = jnp.dot(
                jnp.concatenate(window, axis=1), mats[j], preferred_element_type=jnp.float32
            )
            covered = cover[me, row, j * block // patch_cols]
            out[here, j * block : (j + 1) * block] = value * covered.astype(jnp.float32)
        return carry

    lax.fori_loop(0, rows // LINES, warp, 0)

    gains = smoothing_gains()
    u = (
        lax.broadcasted_iota(jnp.int32, (1, patch_cols), 1).astype(jnp.float32) * (2.0 / patch_cols)
        - (patch_cols - 1) / patch_cols
    )
    weights[...] = jnp.zeros(weights.shape, jnp.float32)
    for q in range(count):
        chosen = index[me, row, q]
        covered = cover[me, row, q].astype(jnp.float32)
        here = slice(EDGE + q * patch_cols, EDGE + (q + 1) * patch_cols)
        for b in range(3):
            terms = []
            for k in range(3):
                sets = [coef[b, k, i, me] for i in range(KSETS)]
                term = sets[0]
                for i in range(1, KSETS):
                    term = jnp.where(chosen == i, sets[i], term)
                terms.append(term * covered * float(gains[b]))
            const, slope, lift = terms
            weights[b : b + 1, here] = const + slope * u
            weights[3 + b : 4 + b, here] = jnp.full((1, patch_cols), lift, jnp.float32)

    def add_model(q):
        def band(r, carry):
            model = band_model(q, r, rows, strip, down, across, weights)
            here = pl.ds(pl.multiple_of(r * BAND, BAND), BAND)
            for there, piece in spans(q, patch_cols, cols):
                out[here, there] -= model[:, piece]
            return carry

        lax.fori_loop(0, rows // BAND, band, 0)

    def halos_in(q):
        for d in range(2):
            @pl.when(halo_there[1 - d])
            def _():
                halo(q, d).wait_recv()

    for b in range(3):
        down[b * BAND : (b + 1) * BAND, :] = banded(b, BAND, BAND + 2 * HALO, HALO)

        def fill(i, carry):
            first = pl.multiple_of(i * HALO, HALO)
            across[b, pl.ds(first, HALO), :] = banded(
                b, HALO, patch_cols + 2 * EDGE, EDGE, i * HALO
            )
            return carry

        lax.fori_loop(0, patch_cols // HALO, fill, 0)

    halos_in(me)
    add_model(me)

    table, digit, per_word, length, finals = codes(count)
    final = pick(me, finals)

    def step(_, words):
        words = list(words)
        code = words[0] % digit
        for w in range(len(words)):
            words[w] = words[w] // digit
            if w + 1 < len(words):
                words[w] = words[w] + (words[w + 1] % digit) * digit ** (per_word - 1)
        kind, event = code % 4, code // 4
        q, c = event // CHUNKS, event % CHUNKS
        onward = paths(me, q, c, count)
        halos = [(c == CHUNKS // 2 * d) & halo_there[d] for d in range(2)]

        @pl.when(kind % 2 == 0)
        def _():
            send(q, c, 0).wait_recv()
            for d in range(2):
                @pl.when(halos[d])
                def _():
                    halo(q, d).start()
            for d in (2, 3, 0, 1):
                @pl.when(onward[d])
                def _():
                    send(q, c, d).start()

        @pl.when(kind == 2)
        def _():
            halos_in(q)

            @pl.when(q != final)
            def _():
                add_model(q)

        @pl.when(kind == 1)
        def _():
            for d in range(4):
                @pl.when(onward[d])
                def _():
                    send(q, c, d).wait_send()
            for d in range(2):
                @pl.when(halos[d])
                def _():
                    halo(q, d).wait_send()

        return tuple(words)

    lax.fori_loop(0, length, step, tuple(pick(me, line) for line in table))


def finish_kernel(count, strip, down, across, weights, value, out, work, far_sem, near_sem):
    rows, cols = value.shape
    patch_cols = strip.shape[2]
    final = pick(lax.axis_index("tile"), codes(count)[-1])
    pieces = spans(final, patch_cols, cols)
    within = (final > 0, final >= 0, final < count - 1)

    def far(q, shift, size):
        here = (slice(None), pl.ds(q * patch_cols + shift, size))
        return pltpu.make_async_copy(value.at[here], out.at[here], far_sem.at[q])

    def near(i, r):
        there, piece = pieces[i]
        return pltpu.make_async_copy(
            work.at[pl.ds(r * BAND, BAND), piece], out.at[pl.ds(r * BAND, BAND), there], near_sem.at[i, r]
        )

    def far_copies(act):
        for q in range(count):
            @pl.when((q < final - 1) | (q > final + 1))
            def _():
                act(far(q, 0, patch_cols))

            @pl.when(q == final - 1)
            def _():
                act(far(q, 0, patch_cols - EDGE))

            @pl.when(q == final + 1)
            def _():
                act(far(q, EDGE, patch_cols - EDGE))

    far_copies(lambda copy: copy.start())
    for r in range(rows // BAND):
        model = band_model(final, r, rows, strip, down, across, weights)
        here = pl.ds(r * BAND, BAND)
        for i, (there, piece) in enumerate(pieces):
            work[here, piece] = value[here, there] - model[:, piece]

            @pl.when(within[i])
            def _():
                near(i, r).start()
    far_copies(lambda copy: copy.wait())
    for r in range(rows // BAND):
        for i in range(3):
            @pl.when(within[i])
            def _():
                near(i, r).wait()


def on_device(exposures, interp, col_offsets, template, coef_table, coef_index, intersection):
    rows, cols = exposures.shape[1:]
    patch_cols = template.shape[1]
    count, ccd_count = lax.axis_size("tile"), lax.axis_size("ccd")
    blocks, depth, block = interp.shape[1:]
    small = [col_offsets, coef_table.transpose(2, 3, 1, 0), coef_index, intersection]

    sources = [
        pltpu.with_memory_space_constraint(array, pltpu.HBM)
        for array in (template, exposures[0], interp[0], *small)
    ]
    in_hbm = pl.BlockSpec(memory_space=pltpu.HBM)
    vmem = pl.BlockSpec(memory_space=pltpu.VMEM)
    shapes = [
        ((rows, cols), jnp.float32),
        ((count, rows + 2 * HALO, patch_cols), jnp.float32),
        ((3 * BAND, BAND + 2 * HALO), jnp.bfloat16),
        ((3, patch_cols, patch_cols + 2 * EDGE), jnp.bfloat16),
        ((8, cols + 2 * EDGE), jnp.float32),
    ]
    value, strip, down, across, weights = pl.pallas_call(
        functools.partial(strip_kernel, count, ccd_count),
        out_shape=[jax.ShapeDtypeStruct(*shape) for shape in shapes],
        in_specs=[in_hbm] * 7,
        out_specs=[vmem] * 5,
        scratch_shapes=[
            pltpu.VMEM((2, LINES, cols), jnp.float32),
            pltpu.VMEM((blocks, LINES, block), jnp.bfloat16),
            pltpu.VMEM((blocks, depth, block), jnp.bfloat16),
            *[pltpu.SMEM(array.shape, array.dtype) for array in small],
            pltpu.SemaphoreType.DMA,
            pltpu.SemaphoreType.DMA((2,)),
            pltpu.SemaphoreType.DMA((5,)),
            pltpu.SemaphoreType.DMA((4, count, CHUNKS)),
            pltpu.SemaphoreType.DMA((count, CHUNKS)),
            pltpu.SemaphoreType.DMA((2, count)),
            pltpu.SemaphoreType.DMA((2, count)),
        ],
        compiler_params=pltpu.CompilerParams(
            collective_id=0, has_side_effects=True, vmem_limit_bytes=16 * 2**20
        ),
    )(*sources)
    result = pl.pallas_call(
        functools.partial(finish_kernel, count),
        out_shape=jax.ShapeDtypeStruct((rows, cols), jnp.float32),
        in_specs=[vmem] * 5,
        out_specs=in_hbm,
        scratch_shapes=[
            pltpu.VMEM((rows, patch_cols + 2 * EDGE), jnp.float32),
            pltpu.SemaphoreType.DMA((count,)),
            pltpu.SemaphoreType.DMA((3, rows // BAND)),
        ],
        compiler_params=pltpu.CompilerParams(vmem_limit_bytes=16 * 2**20),
    )(strip, down, across, weights, value)
    return result[None]


def solution(mesh):
    placed = (
        P("tile", "ccd", None),
        P("tile", None, None, None),
        P("tile", None),
        P("ccd", "tile"),
        P(),
        P(),
        P(),
    )
    return jax.shard_map(
        on_device, mesh=mesh, in_specs=placed, out_specs=P("tile", "ccd", None), check_vma=False
    )
```

```python
import functools
import heapq

import jax
import jax.numpy as jnp
import ml_dtypes
import numpy as np
from jax import lax
from jax.experimental import pallas as pl
from jax.experimental.pallas import tpu as pltpu
from jax.sharding import PartitionSpec as P

HALF = 10
KSETS = 4
SIGMAS = (1.5, 3.0, 5.0)
HALO = 16
EDGE = 128
BAND = 128
MARGIN = 1
NOTHING = 3
CHUNKS = 4
LINES = 128


def basis_taps():
    positions = np.arange(-HALF, HALF + 1).astype(np.float64)
    kernels = []
    for sigma_value in SIGMAS:
        gauss = np.exp(-0.5 * (positions / sigma_value) ** 2)
        kernels.append(gauss / np.sum(gauss))
    return kernels


def smoothing_gains():
    near = [taps.astype(ml_dtypes.bfloat16).astype(np.float64) for taps in basis_taps()]
    return [1.0 / np.sum(taps) ** 2 for taps in near]


def banded(b, rows, cols, shift, first=0):
    shape = (rows, cols)
    distance = (
        lax.broadcasted_iota(jnp.int32, shape, 1)
        - lax.broadcasted_iota(jnp.int32, shape, 0)
        - (shift + first)
    )
    away = distance.astype(jnp.float32)
    taps = jnp.exp(away * away * (-0.5 / SIGMAS[b] ** 2)) * basis_taps()[b][HALF]
    return jnp.where(jnp.abs(away) <= HALF, taps, 0.0).astype(jnp.bfloat16)


def inner_size(count):
    best = 1
    for size in range(1, count + 1):
        if count % size == 0 and size * size <= count:
            best = size
    return best


def turns(d, qz, c, outer):
    late = c >= CHUNKS // 2
    ends = ((d == 0) & (qz == outer - 1)) | ((d == outer - 1) & (qz == 0))
    inside = (d > 0) & (d < outer - 1) & ((qz == d - 1) | (qz == d + 1))
    return (ends & late) | (inside & (late | (qz == 0) | (qz == outer - 1)))


def paths(me, q, c, count):
    inner = inner_size(count)
    outer = count // inner
    z, x = me // inner, me % inner
    qz, qx = q // inner, q % inner
    own = qx == x
    across = (qz == z) | (turns(z, qz, c, outer) ^ True)
    return (
        (z > 0) & (qz >= z) & (own | turns(z - 1, qz, c, outer)),
        (z < outer - 1) & (qz <= z) & (own | turns(z + 1, qz, c, outer)),
        across & (qx >= x) & (x > 0),
        across & (qx <= x) & (x < inner - 1),
    )


def place(c):
    half = CHUNKS // 2
    return c + (c // half) * (CHUNKS + half - 1 - 2 * c)


def programs(count):
    inner = inner_size(count)
    steps = (-inner, inner, -1, 1)
    free, order = {}, 0
    queue = [(0, False, me, me, c, me * CHUNKS + c) for me in range(count) for c in range(CHUNKS)]
    order = len(queue)
    heapq.heapify(queue)
    arrivals = [[] for _ in range(count)]
    drains = [[] for _ in range(count)]
    while queue:
        time, _, me, q, c, _ = heapq.heappop(queue)
        if q != me:
            arrivals[me].append((time, q * CHUNKS + c))
        sent = [time] if c % (CHUNKS // 2) == 0 else []
        for d, go in enumerate(paths(me, q, c, count)):
            if go:
                done = max(free.get((me, d), 0), time) + 1
                free[me, d] = done
                sent.append(done)
                to = me + steps[d]
                heapq.heappush(queue, (done, (q - to) % inner != 0, to, q, c, order))
                order += 1
        if sent:
            drains[me].append((max(sent) + MARGIN, q * CHUNKS + c))
    result = []
    for me in range(count):
        left = {q: CHUNKS for q in range(count)}
        steps = []
        for i, (time, event) in enumerate(arrivals[me]):
            left[event // CHUNKS] -= 1
            steps.append((time, 0, i, event * 4 + 2 * (left[event // CHUNKS] == 0)))
        for i, (time, event) in enumerate(drains[me]):
            steps.append((time, 1, i, event * 4 + 1))
        result.append([step[-1] for step in sorted(steps)])
    longest = max(len(steps) for steps in result)
    finals = [arrivals[me][-1][1] // CHUNKS for me in range(count)]
    return [[NOTHING] * (longest - len(steps)) + steps for steps in result], finals


def pick(me, values):
    value = jnp.int32(values[0])
    for i in range(1, len(values)):
        value = jnp.where(me == i, jnp.int32(values[i]), value)
    return value


def codes(count):
    bits = (count * CHUNKS * 4 - 1).bit_length()
    digit, per_word = 2**bits, 30 // bits
    steps, finals = programs(count)
    words = [
        [sum(v * digit**i for i, v in enumerate(line[first : first + per_word])) for line in steps]
        for first in range(0, len(steps[0]), per_word)
    ]
    return words, digit, per_word, len(steps[0]), finals


def spans(q, patch_cols, cols):
    first = pl.multiple_of(q * patch_cols, EDGE)
    left = pl.multiple_of(jnp.maximum(first - EDGE, 0), EDGE)
    right = pl.multiple_of(jnp.minimum(first + patch_cols, cols - EDGE), EDGE)
    return (
        (pl.ds(left, EDGE), slice(0, EDGE)),
        (pl.ds(first, patch_cols), slice(EDGE, EDGE + patch_cols)),
        (pl.ds(right, EDGE), slice(EDGE + patch_cols, 2 * EDGE + patch_cols)),
    )


def band_model(q, r, rows, strip, down, across, weights):
    patch_cols = strip.shape[2]
    first = pl.multiple_of(q * patch_cols, EDGE)
    wide = patch_cols + 2 * EDGE
    at = pl.multiple_of(r * BAND, BAND)
    pixel = strip[q, pl.ds(at, BAND + 2 * HALO), :].astype(jnp.bfloat16)
    tall = jnp.dot(down[...], pixel, preferred_element_type=jnp.float32)
    tall = tall.astype(jnp.bfloat16)
    v = (
        lax.broadcasted_iota(jnp.int32, (BAND, wide), 0) + r * BAND
    ).astype(jnp.float32) * (2.0 / rows) - (rows - 1) / rows
    model = None
    for b in range(3):
        parts = []
        for at in range(0, wide, 2 * EDGE):
            low = max(0, at - EDGE - HALF) // EDGE * EDGE
            high = min(patch_cols, -(-(at + EDGE + HALF) // EDGE) * EDGE)
            parts.append(jnp.dot(
                tall[b * BAND : (b + 1) * BAND, low:high],
                across[b, low:high, at : at + 2 * EDGE],
                preferred_element_type=jnp.float32,
            ))
        flat = jnp.concatenate(parts, axis=1)
        const = weights[b : b + 1, pl.ds(first, wide)]
        slope = weights[3 + b : 4 + b, pl.ds(first, wide)]
        term = (const + slope * v) * flat
        model = term if model is None else model + term
    return model


def strip_kernel(
    count, ccd_count, template, exposure, interp, offset_in, coef_in, index_in, cover_in,
    out, strip, down, across, weights, lines, pixels, mats, offsets, coef, index, cover,
    load_sem, line_sem, small_sem, send_sem, recv_sem, hsend_sem, hrecv_sem,
):
    me = lax.axis_index("tile")
    row = lax.axis_index("ccd")
    inner = inner_size(count)
    outer = count // inner
    z, x = me // inner, me % inner
    rows, patch_cols = template.shape
    cols = out.shape[1]
    part = rows // CHUNKS

    targets = (me - inner, me + inner, me - 1, me + 1)
    there = (z > 0, z < outer - 1, x > 0, x < inner - 1)
    halo_there = (row > 0, row < ccd_count - 1)

    load = pltpu.make_async_copy(template, strip.at[me, pl.ds(HALO, rows)], load_sem)
    load.start()

    barrier = pltpu.get_barrier_semaphore()
    total = jnp.int32(0)
    for target, exists in zip(targets, there):
        @pl.when(exists)
        def _():
            pl.semaphore_signal(barrier, inc=1, device_id=(row, target))
        total = total + exists.astype(jnp.int32)
    for step, exists in zip((-1, 1), halo_there):
        @pl.when(exists)
        def _():
            pl.semaphore_signal(barrier, inc=1, device_id=(row + step, me))
        total = total + exists.astype(jnp.int32)

    load.wait()
    pl.semaphore_wait(barrier, total)

    def send(q, c, d):
        first = place(c) * part
        piece = pl.ds(pl.multiple_of(HALO + first, HALO), part)
        return pltpu.make_async_remote_copy(
            src_ref=strip.at[q, piece],
            dst_ref=strip.at[q, piece],
            send_sem=send_sem.at[d, q, c],
            recv_sem=recv_sem.at[q, c],
            device_id=(row, targets[d]),
        )

    def halo(q, d):
        source = pl.ds(HALO, HALO) if d == 0 else pl.ds(rows, HALO)
        target = pl.ds(HALO + rows, HALO) if d == 0 else pl.ds(0, HALO)
        return pltpu.make_async_remote_copy(
            src_ref=strip.at[q, source],
            dst_ref=strip.at[q, target],
            send_sem=hsend_sem.at[d, q],
            recv_sem=hrecv_sem.at[d, q],
            device_id=(row + (-1 if d == 0 else 1), me),
        )

    for c in range(CHUNKS):
        for d in (2, 3, 0, 1):
            @pl.when(there[d])
            def _():
                send(me, c, d).start()
    small = [
        pltpu.make_async_copy(source, target, small_sem.at[i])
        for i, (source, target) in enumerate(
            [(offset_in, offsets), (coef_in, coef), (index_in, index), (cover_in, cover), (interp, mats)]
        )
    ]
    for copy in small:
        copy.start()

    def line_copy(i, slot):
        return pltpu.make_async_copy(
            exposure.at[pl.ds(pl.multiple_of(i * LINES, LINES), LINES)], lines.at[slot], line_sem.at[slot]
        )

    line_copy(0, 0).start()
    for d in range(2):
        @pl.when(halo_there[d])
        def _():
            halo(me, d).start()

    @pl.when(row == 0)
    def _():
        for q in range(count):
            strip[q, 0:HALO, :] = jnp.zeros((HALO, patch_cols), jnp.float32)

    @pl.when(row == ccd_count - 1)
    def _():
        for q in range(count):
            strip[q, rows + HALO : rows + 2 * HALO, :] = jnp.zeros((HALO, patch_cols), jnp.float32)

    for copy in small:
        copy.wait()

    blocks, depth, block = mats.shape

    def warp(i, carry):
        slot = i % 2
        line_copy(i, slot).wait()

        @pl.when(i + 1 < rows // LINES)
        def _():
            line_copy(i + 1, 1 - slot).start()

        for j in range(blocks):
            pixels[j] = lines[slot, :, j * block : (j + 1) * block].astype(jnp.bfloat16)
        here = pl.ds(pl.multiple_of(i * LINES, LINES), LINES)
        for j in range(blocks):
            start = offsets[0, j]
            window = [pixels[start + k] for k in range(depth // block)]
            value = jnp.dot(
                jnp.concatenate(window, axis=1), mats[j], preferred_element_type=jnp.float32
            )
            covered = cover[me, row, j * block // patch_cols]
            out[here, j * block : (j + 1) * block] = value * covered.astype(jnp.float32)
        return carry

    lax.fori_loop(0, rows // LINES, warp, 0)

    gains = smoothing_gains()
    u = (
        lax.broadcasted_iota(jnp.int32, (1, patch_cols), 1).astype(jnp.float32) * (2.0 / patch_cols)
        - (patch_cols - 1) / patch_cols
    )
    weights[...] = jnp.zeros(weights.shape, jnp.float32)
    for q in range(count):
        chosen = index[me, row, q]
        covered = cover[me, row, q].astype(jnp.float32)
        here = slice(EDGE + q * patch_cols, EDGE + (q + 1) * patch_cols)
        for b in range(3):
            terms = []
            for k in range(3):
                sets = [coef[b, k, i, me] for i in range(KSETS)]
                term = sets[0]
                for i in range(1, KSETS):
                    term = jnp.where(chosen == i, sets[i], term)
                terms.append(term * covered * float(gains[b]))
            const, slope, lift = terms
            weights[b : b + 1, here] = const + slope * u
            weights[3 + b : 4 + b, here] = jnp.full((1, patch_cols), lift, jnp.float32)

    def add_model(q):
        def band(r, carry):
            model = band_model(q, r, rows, strip, down, across, weights)
            here = pl.ds(pl.multiple_of(r * BAND, BAND), BAND)
            for there, piece in spans(q, patch_cols, cols):
                out[here, there] -= model[:, piece]
            return carry

        lax.fori_loop(0, rows // BAND, band, 0)

    def halos_in(q):
        for d in range(2):
            @pl.when(halo_there[1 - d])
            def _():
                halo(q, d).wait_recv()

    for b in range(3):
        down[b * BAND : (b + 1) * BAND, :] = banded(b, BAND, BAND + 2 * HALO, HALO)

        def fill(i, carry):
            first = pl.multiple_of(i * HALO, HALO)
            across[b, pl.ds(first, HALO), :] = banded(
                b, HALO, patch_cols + 2 * EDGE, EDGE, i * HALO
            )
            return carry

        lax.fori_loop(0, patch_cols // HALO, fill, 0)

    halos_in(me)
    add_model(me)

    table, digit, per_word, length, finals = codes(count)
    final = pick(me, finals)

    def step(_, words):
        words = list(words)
        code = words[0] % digit
        for w in range(len(words)):
            words[w] = words[w] // digit
            if w + 1 < len(words):
                words[w] = words[w] + (words[w + 1] % digit) * digit ** (per_word - 1)
        kind, event = code % 4, code // 4
        q, c = event // CHUNKS, event % CHUNKS
        onward = paths(me, q, c, count)
        halos = [(c == CHUNKS // 2 * d) & halo_there[d] for d in range(2)]

        @pl.when(kind % 2 == 0)
        def _():
            send(q, c, 0).wait_recv()
            for d in range(2):
                @pl.when(halos[d])
                def _():
                    halo(q, d).start()
            for d in (2, 3, 0, 1):
                @pl.when(onward[d])
                def _():
                    send(q, c, d).start()

        @pl.when(kind == 2)
        def _():
            halos_in(q)

            @pl.when(q != final)
            def _():
                add_model(q)

        @pl.when(kind == 1)
        def _():
            for d in range(4):
                @pl.when(onward[d])
                def _():
                    send(q, c, d).wait_send()
            for d in range(2):
                @pl.when(halos[d])
                def _():
                    halo(q, d).wait_send()

        return tuple(words)

    lax.fori_loop(0, length, step, tuple(pick(me, line) for line in table))


def finish_kernel(count, strip, down, across, weights, value, out, work, far_sem, near_sem):
    rows, cols = value.shape
    patch_cols = strip.shape[2]
    final = pick(lax.axis_index("tile"), codes(count)[-1])
    pieces = spans(final, patch_cols, cols)
    within = (final > 0, final >= 0, final < count - 1)

    def far(q, shift, size):
        here = (slice(None), pl.ds(q * patch_cols + shift, size))
        return pltpu.make_async_copy(value.at[here], out.at[here], far_sem.at[q])

    def near(i, r):
        there, piece = pieces[i]
        return pltpu.make_async_copy(
            work.at[pl.ds(r * BAND, BAND), piece], out.at[pl.ds(r * BAND, BAND), there], near_sem.at[i, r]
        )

    def far_copies(act):
        for q in range(count):
            @pl.when((q < final - 1) | (q > final + 1))
            def _():
                act(far(q, 0, patch_cols))

            @pl.when(q == final - 1)
            def _():
                act(far(q, 0, patch_cols - EDGE))

            @pl.when(q == final + 1)
            def _():
                act(far(q, EDGE, patch_cols - EDGE))

    far_copies(lambda copy: copy.start())
    for r in range(rows // BAND):
        model = band_model(final, r, rows, strip, down, across, weights)
        here = pl.ds(r * BAND, BAND)
        for i, (there, piece) in enumerate(pieces):
            work[here, piece] = value[here, there] - model[:, piece]

            @pl.when(within[i])
            def _():
                near(i, r).start()
    far_copies(lambda copy: copy.wait())
    for r in range(rows // BAND):
        for i in range(3):
            @pl.when(within[i])
            def _():
                near(i, r).wait()


def on_device(exposures, interp, col_offsets, template, coef_table, coef_index, intersection):
    rows, cols = exposures.shape[1:]
    patch_cols = template.shape[1]
    count, ccd_count = lax.axis_size("tile"), lax.axis_size("ccd")
    blocks, depth, block = interp.shape[1:]
    small = [col_offsets, coef_table.transpose(2, 3, 1, 0), coef_index, intersection]

    sources = [
        pltpu.with_memory_space_constraint(array, pltpu.HBM)
        for array in (template, exposures[0], interp[0], *small)
    ]
    in_hbm = pl.BlockSpec(memory_space=pltpu.HBM)
    vmem = pl.BlockSpec(memory_space=pltpu.VMEM)
    shapes = [
        ((rows, cols), jnp.float32),
        ((count, rows + 2 * HALO, patch_cols), jnp.float32),
        ((3 * BAND, BAND + 2 * HALO), jnp.bfloat16),
        ((3, patch_cols, patch_cols + 2 * EDGE), jnp.bfloat16),
        ((8, cols + 2 * EDGE), jnp.float32),
    ]
    value, strip, down, across, weights = pl.pallas_call(
        functools.partial(strip_kernel, count, ccd_count),
        out_shape=[jax.ShapeDtypeStruct(*shape) for shape in shapes],
        in_specs=[in_hbm] * 7,
        out_specs=[vmem] * 5,
        scratch_shapes=[
            pltpu.VMEM((2, LINES, cols), jnp.float32),
            pltpu.VMEM((blocks, LINES, block), jnp.bfloat16),
            pltpu.VMEM((blocks, depth, block), jnp.bfloat16),
            *[pltpu.SMEM(array.shape, array.dtype) for array in small],
            pltpu.SemaphoreType.DMA,
            pltpu.SemaphoreType.DMA((2,)),
            pltpu.SemaphoreType.DMA((5,)),
            pltpu.SemaphoreType.DMA((4, count, CHUNKS)),
            pltpu.SemaphoreType.DMA((count, CHUNKS)),
            pltpu.SemaphoreType.DMA((2, count)),
            pltpu.SemaphoreType.DMA((2, count)),
        ],
        compiler_params=pltpu.CompilerParams(
            collective_id=0, has_side_effects=True, vmem_limit_bytes=16 * 2**20
        ),
    )(*sources)
    result = pl.pallas_call(
        functools.partial(finish_kernel, count),
        out_shape=jax.ShapeDtypeStruct((rows, cols), jnp.float32),
        in_specs=[vmem] * 5,
        out_specs=in_hbm,
        scratch_shapes=[
            pltpu.VMEM((rows, patch_cols + 2 * EDGE), jnp.float32),
            pltpu.SemaphoreType.DMA((count,)),
            pltpu.SemaphoreType.DMA((3, rows // BAND)),
        ],
        compiler_params=pltpu.CompilerParams(vmem_limit_bytes=16 * 2**20),
    )(strip, down, across, weights, value)
    return result[None]


def solution(mesh):
    placed = (
        P("tile", "ccd", None),
        P("tile", None, None, None),
        P("tile", None),
        P("ccd", "tile"),
        P(),
        P(),
        P(),
    )
    return jax.shard_map(
        on_device, mesh=mesh, in_specs=placed, out_specs=P("tile", "ccd", None), check_vma=False
    )
```
